256 devices in a mesh: prow: 8 (over y, core), pcol: 32 (over z, x).
Axes of the slice: x: 4, y: 4, z: 8, core: 2. Of those that a mesh axis runs over, the one named last changes fastest.
Arguments:
- matrix: float32 [4096, 16384], P('prow', 'pcol'), may hold values from -6 to 6
- pivots_first: int32 [512], replicated, may hold values from 512 to 4095, as said below
- pivots_second: int32 [512], replicated, may hold values from 1024 to 4095, as said below
- lower_first: float32 [512, 512], replicated, as said below
- upper_first: float32 [512, 512], replicated, as said below
- lower_second: float32 [512, 512], replicated, as said below
- upper_second: float32 [512, 512], replicated, as said below
Outputs:
- factored: float32 [4096, 16384], P('prow', 'pcol')
The draws below stay inside these ranges and needn't reach their ends.
Inputs may be any that keep to these rules, and one draw needn't show every extreme that they name: `pivots_first`: 512 distinct working-order row indices; both the smallest and the largest allowed value occur. `pivots_second`: 512 distinct working-order row indices; both the smallest and the largest allowed value occur. `lower_first`: unit lower triangular. `upper_first`: upper triangular with a positive diagonal. `lower_second`: unit lower triangular. `upper_second`: upper triangular with a positive diagonal.
All inputs are finite; a program needn't handle non-finite values.
Results may differ from the reference program's by a relative error of at most 0.00009.
Values sent between devices are 32-bit elements; how exact they have to be, the bound alone decides.
A program may use at most 64 MiB of HBM per device.

```python
import math
import jax
import jax.numpy as jnp
from jax import lax

NB = 512
RB = 1
CB = 1
ROWS = 4096
COLS = 16384
N_PROW = 8
N_PCOL = 32


def pick_pivots(key, lowest):
    span = ROWS - lowest - 2
    middle = jax.random.permutation(key, span)[:NB - 2].astype(jnp.int32) + lowest + 1
    ends = jnp.array([lowest, ROWS - 1], dtype=jnp.int32)
    chosen = jnp.concatenate([ends, middle])
    order = jax.random.permutation(jax.random.fold_in(key, 7), NB)
    return chosen[order]


def draw_pivots_first(key, part):
    key = jax.random.fold_in(key, 1)
    return pick_pivots(key, NB)


def draw_pivots_second(key, part):
    key = jax.random.fold_in(key, 2)
    return pick_pivots(key, 2 * NB)


def unit_lower(noise):
    return jnp.tril(noise * (0.4 / math.sqrt(NB)), -1) + jnp.eye(NB, dtype=jnp.float32)


def scaled_upper(noise, diag_values):
    factor = 1.0 / math.sqrt(NB)
    return jnp.triu(noise * (0.4 * factor / math.sqrt(NB)), 1) + jnp.diag(diag_values * factor)


def draw_lower_first(key, part):
    key = jax.random.fold_in(key, 3)
    noise = jax.random.normal(key, (NB, NB), jnp.float32)
    return unit_lower(noise)


def draw_lower_second(key, part):
    key = jax.random.fold_in(key, 4)
    noise = jax.random.normal(key, (NB, NB), jnp.float32)
    return unit_lower(noise)


def draw_upper_first(key, part):
    key = jax.random.fold_in(key, 5)
    diag_values = jax.random.uniform(jax.random.fold_in(key, 9), (NB,), jnp.float32, 0.5, 1.5)
    noise = jax.random.normal(key, (NB, NB), jnp.float32)
    return scaled_upper(noise, diag_values)


def draw_upper_second(key, part):
    key = jax.random.fold_in(key, 6)
    diag_values = jax.random.uniform(jax.random.fold_in(key, 9), (NB,), jnp.float32, 0.5, 1.5)
    noise = jax.random.normal(key, (NB, NB), jnp.float32)
    return scaled_upper(noise, diag_values)


def block_levels(stream_key, shape, split, low, high):
    level = 1.0
    for position, shards_of in split:
        draws = jax.random.uniform(jax.random.fold_in(jax.random.fold_in(stream_key, 6), position), (shards_of,), jnp.float32, low / len(split), high / len(split))
        level = level * jnp.repeat(jnp.exp(draws), shape[position] // shards_of).reshape((-1,) + (1,) * (len(shape) - 1 - position))
    return level


def centred(own_key, shape, scale, most, split=(), kind=jnp.bfloat16):
    level = block_levels(own_key, shape, split, -0.22, 0.18) if split else 1.0
    result = jax.random.normal(own_key, shape, jnp.float32) * scale * level
    return jnp.minimum(jnp.maximum(result, -most), most).astype(kind)


def setup_inputs(seed: int = 0) -> dict:
    splits = jax.random.split(jax.random.key(seed), 8)
    return {
        "matrix": centred(splits[0], (ROWS, COLS), 1.0, 6.0, ((0, 8), (1, 32)), jnp.float32),
        "pivots_first": draw_pivots_first(jax.random.fold_in(splits[7], 71), 0),
        "pivots_second": draw_pivots_second(jax.random.fold_in(splits[7], 71), 0),
        "lower_first": draw_lower_first(jax.random.fold_in(splits[7], 71), 0),
        "upper_first": draw_upper_first(jax.random.fold_in(splits[7], 71), 0),
        "lower_second": draw_lower_second(jax.random.fold_in(splits[7], 71), 0),
        "upper_second": draw_upper_second(jax.random.fold_in(splits[7], 71), 0),
    }


def to_working(stored):
    rows = stored.reshape(N_PROW, RB, NB, COLS).transpose(1, 0, 2, 3).reshape(ROWS, COLS)
    return rows.reshape(ROWS, N_PCOL, CB, NB).transpose(0, 2, 1, 3).reshape(ROWS, COLS)


def to_stored(working):
    cols = working.reshape(ROWS, CB, N_PCOL, NB).transpose(0, 2, 1, 3).reshape(ROWS, COLS)
    return cols.reshape(RB, N_PROW, NB, COLS).transpose(1, 0, 2, 3).reshape(ROWS, COLS)


def product(left, right):
    return jnp.dot(left, right, precision=lax.Precision.HIGHEST, preferred_element_type=jnp.float32)


def eliminate(work, pivots, lower, upper, step):
    top = step * NB
    edge = top + NB
    old_top = work[top:edge]
    new_top = work[pivots]
    work = work.at[pivots].set(old_top)
    work = work.at[top:edge].set(new_top)
    panel = product(work[edge:, top:edge], upper)
    urows = product(lower, work[top:edge, edge:])
    work = work.at[edge:, top:edge].set(panel)
    work = work.at[top:edge, edge:].set(urows)
    work = work.at[edge:, edge:].add(-product(panel, urows))
    return work


def reference(matrix, pivots_first, pivots_second, lower_first, upper_first, lower_second, upper_second):
    work = to_working(matrix)
    work = eliminate(work, pivots_first, lower_first, upper_first, 0)
    work = eliminate(work, pivots_second, lower_second, upper_second, 1)
    return to_stored(work)
```

```python
import functools

import jax
import jax.numpy as jnp
from jax import lax
from jax.experimental import pallas as pl
from jax.experimental.pallas import tpu as pltpu
from jax.sharding import PartitionSpec as P

MESH = pl.DeviceIdType.MESH
NB = 512
HALF = NB // 2
NY, NC, NZ, NX = 4, 2, 8, 4
PART = NB // NX
SUBS = 2
SUB = PART // SUBS
WCH = 4
WROWS = HALF // WCH
F32 = jnp.float32
BF16 = jnp.bfloat16


def dot1(a, b):
    return jnp.dot(a, b, preferred_element_type=F32)


def split2(a):
    high = a.astype(BF16)
    return high, (a - high.astype(F32)).astype(BF16)


def split3(a):
    high = a.astype(BF16)
    rest = a - high.astype(F32)
    mid = rest.astype(BF16)
    return high, mid, (rest - mid.astype(F32)).astype(BF16)


def product(a, b):
    ah, al = split2(a)
    bh, bl = split2(b)
    return dot1(ah, bh) + (dot1(ah, bl) + dot1(al, bh))


def pick(onehot, parts):
    high, mid, low = parts
    return dot1(onehot, high) + (dot1(onehot, mid) + dot1(onehot, low))


def onehot_of(source, first):
    lanes = lax.broadcasted_iota(jnp.int32, (NB, NB), 1).astype(F32) + first
    return jnp.where(source == lanes, 1.0, 0.0).astype(BF16)


def kernel(
    w_ref, pf_ref, ps_ref, l0_hbm, u0_hbm, l1_hbm, u1_hbm, out_ref,
    l0, u0, l1, u1, xp, sib, hs, rsr, xf, wb, xi, px0, px1, c10, c01, li0, ur0, f1,
    fac_sem, sib_s, sib_r, w_s, w_r, ws_s, ws_r, rs_s, rs_r, ag_s, ag_r, as_s, as_r,
    a_s, a_r, b_s, b_r, c_s, c_r, cs_s, cs_r,
):
    prow = lax.axis_index("prow")
    pcol = lax.axis_index("pcol")
    y, h = prow // 2, prow % 2
    z, x = pcol // NX, pcol % NX
    other = 1 - h

    def at(dy=0, dc=0, dz=0, dx=0):
        return {
            "prow": ((y + dy + NY) % NY) * NC + (h + dc) % NC,
            "pcol": ((z + dz + NZ) % NZ) * NX + (x + dx + NX) % NX,
        }

    sibling = at(dc=1)
    pending = []

    def when(cond, fn):
        if cond is None:
            fn()
        else:
            pl.when(cond)(fn)

    def send(src, dst, ssem, rsem, device, cond=None):
        copy = pltpu.make_async_remote_copy(
            src_ref=src, dst_ref=dst, send_sem=ssem, recv_sem=rsem, device_id=device, device_id_type=MESH
        )
        when(cond, copy.start)
        pending.append((cond, copy))

    def await_recv(dst, ssem, rsem, cond=None):
        copy = pltpu.make_async_remote_copy(
            src_ref=dst, dst_ref=dst, send_sem=ssem, recv_sem=rsem, device_id=sibling, device_id_type=MESH
        )
        when(cond, copy.wait_recv)

    factors = [
        pltpu.make_async_copy(src, dst, fac_sem.at[k])
        for k, (src, dst) in enumerate(((l0_hbm, l0), (u0_hbm, u0), (l1_hbm, l1), (u1_hbm, u1)))
    ]
    for copy in factors:
        copy.start()

    partners = [
        at(dc=1), at(dy=1), at(dy=2), at(dy=3), at(dx=1), at(dx=2), at(dx=3),
        at(dz=1), at(dz=2), at(dz=-1), at(dz=-2),
    ]
    barrier = pltpu.get_barrier_semaphore()
    for partner in partners:
        pl.semaphore_signal(barrier, inc=1, device_id=partner, device_id_type=MESH)
    pl.semaphore_wait(barrier, len(partners))

    top = y == 0

    def wslice(way, k):
        return wb.at[h, pl.ds(way * HALF + k * WROWS, WROWS)]

    for k in range(WCH):
        for way, dy in ((0, 1), (1, -1)):
            rows = pl.ds(way * HALF + k * WROWS, WROWS)
            send(w_ref.at[rows], wslice(way, k), w_s.at[way, k], w_r.at[way, k], at(dy=dy), top)

    base = (prow * NB).astype(F32)
    pf_row = pf_ref[...].astype(F32)
    ps_row = ps_ref[...].astype(F32)
    row_id = lax.broadcasted_iota(jnp.int32, (NB, NB), 0).astype(F32)
    col_id = lax.broadcasted_iota(jnp.int32, (NB, NB), 1).astype(F32)
    diagonal = row_id == col_id
    pf_col = jnp.sum(jnp.where(diagonal, pf_row, 0.0), axis=1, keepdims=True)
    ps_col = jnp.sum(jnp.where(diagonal, ps_row, 0.0), axis=1, keepdims=True)
    chained = jnp.sum(jnp.where(ps_col == pf_row, col_id + 1.0, 0.0), axis=1, keepdims=True)
    src1 = jnp.where(chained > 0.0, chained - 1.0, ps_col)

    w_parts = split3(w_ref[...])
    xp[0:NB] = pick(onehot_of(pf_col, base), w_parts)
    far = pl.multiple_of(other * HALF, HALF)
    near = pl.multiple_of(h * HALF, HALF)
    send(xp.at[0:NB, pl.ds(far, HALF)], sib.at[0:NB], sib_s.at[0], sib_r.at[0], sibling)
    xp[NB:] = pick(onehot_of(src1, base), w_parts)
    send(xp.at[NB:, pl.ds(far, HALF)], sib.at[NB:], sib_s.at[1], sib_r.at[1], sibling)

    for k in range(2):
        rows = pl.ds(k * NB, NB)
        await_recv(sib.at[rows], sib_s.at[k], sib_r.at[k])
        hs[rows] = xp[rows, pl.ds(near, HALF)] + sib[rows]

    def chunk(c):
        return pl.ds(pl.multiple_of(c * HALF, HALF), HALF)

    for d in range(1, NY):
        send(hs.at[chunk((y + d) % NY)], rsr.at[d - 1], rs_s.at[d - 1], rs_r.at[d - 1], at(dy=d))

    def relay_all(order):
        for way, k in order:
            ref = wslice(way, k)
            await_recv(ref, w_s.at[way, k], w_r.at[way, k])
            hop = y if way == 0 else NY - y
            onward = pltpu.make_async_remote_copy(
                src_ref=ref, dst_ref=ref, send_sem=w_s.at[way, k], recv_sem=w_r.at[way, k],
                device_id=at(dy=1 - 2 * way), device_id_type=MESH,
            )
            pl.when(hop < NY - 1)(onward.start)
            pltpu.make_async_remote_copy(
                src_ref=ref, dst_ref=ref, send_sem=ws_s.at[way, k], recv_sem=ws_r.at[way, k],
                device_id=sibling, device_id_type=MESH,
            ).start()

    first = [(0, k) for k in range(WCH)]
    second = [(1, k) for k in range(WCH)]
    mixed = [(way, k) for k in range(WCH) for way in range(2)]
    pl.when(y == 1)(lambda: relay_all(first + second))
    pl.when(y == 2)(lambda: relay_all(mixed))
    pl.when(y == 3)(lambda: relay_all(second + first))
    below = y > 0
    for way, k in mixed:
        ref = wslice(way, k)
        hop = y if way == 0 else NY - y
        onward = pltpu.make_async_remote_copy(
            src_ref=ref, dst_ref=ref, send_sem=w_s.at[way, k], recv_sem=w_r.at[way, k],
            device_id=at(dy=1 - 2 * way), device_id_type=MESH,
        )
        pending.append((jnp.logical_and(below, hop < NY - 1), onward))
        across = pltpu.make_async_remote_copy(
            src_ref=ref, dst_ref=ref, send_sem=ws_s.at[way, k], recv_sem=ws_r.at[way, k],
            device_id=sibling, device_id_type=MESH,
        )
        pending.append((below, across))

    mine = chunk(y)
    for d in range(1, NY):
        await_recv(rsr.at[d - 1], rs_s.at[d - 1], rs_r.at[d - 1])
    xf[h, mine] = (hs[mine] + rsr[0]) + (rsr[1] + rsr[2])
    for d in range(1, NY):
        send(xf.at[h, mine], xf.at[h, mine], ag_s.at[d - 1], ag_r.at[d - 1], at(dy=d))
    send(xf.at[h, mine], xf.at[h, mine], as_s.at[0], as_r.at[0], sibling)

    def place_rows():
        for way, k in mixed:
            ref = wb.at[other, pl.ds(way * HALF + k * WROWS, WROWS)]
            await_recv(ref, ws_s.at[way, k], ws_r.at[way, k])
        here = base + row_id[:, 0:1]
        moved = jnp.sum(jnp.where(pf_row == here, col_id + 1.0, 0.0), axis=1, keepdims=True)
        under = col_id + float(NB)
        linked = jnp.sum(jnp.where(pf_col == under, row_id + 1.0, 0.0), axis=0, keepdims=True)
        origin = jnp.where(linked > 0.0, linked, under[0:1] + 1.0)
        taken = jnp.sum(jnp.where(ps_row == here, origin, 0.0), axis=1, keepdims=True)
        source = jnp.where(taken > 0.0, taken, moved) - 1.0
        incoming = pick(onehot_of(source, 0.0), split3(wb[0]))
        incoming += pick(onehot_of(source, float(NB)), split3(wb[1]))
        xi[...] = jnp.where(source < 0.0, w_ref[...], incoming)

    pl.when(below)(place_rows)

    def keep_panel(panel):
        panel[...] = xi[...]

    pl.when(jnp.logical_and(below, pcol == 0))(lambda: keep_panel(px0))
    pl.when(jnp.logical_and(below, pcol == 1))(lambda: keep_panel(px1))

    units = [(b, s) for b in range(4) for s in range(SUBS)]

    def rows_of(unit, part):
        b, s = unit
        rows = pl.ds(pl.multiple_of(part * PART + s * SUB, SUB), SUB)
        return (px0.at[rows], px1.at[rows], c10.at[h, rows], c01.at[h, rows])[b]

    def both(*conds):
        conds = [c for c in conds if c is not None]
        return functools.reduce(jnp.logical_and, conds) if conds else None

    row0 = z == 0

    def scatter_parts(chosen):
        for u, unit in chosen:
            root = unit[0] % 2
            plane = below if unit[0] < 2 else None
            for d in range(1, NX):
                ref = rows_of(unit, (root + d) % NX)
                send(ref, ref, a_s.at[u, d - 1], a_r.at[u], at(dx=d), both(plane, pcol == root))

    def spread(chosen):
        for u, unit in chosen:
            root = unit[0] % 2
            plane = below if unit[0] < 2 else None
            ref = rows_of(unit, x)
            await_recv(ref, a_s.at[u, 0], a_r.at[u], both(plane, row0, x != root))
            await_recv(ref, b_s.at[u, 0], b_r.at[u], both(plane, z != 0))
            up = both(plane, jnp.logical_or(row0, z == 2))
            down = both(plane, jnp.logical_or(row0, z == 6))
            send(ref, ref, b_s.at[u, 0], b_r.at[u], at(dz=1), up)
            send(ref, ref, b_s.at[u, 1], b_r.at[u], at(dz=2), up)
            send(ref, ref, b_s.at[u, 2], b_r.at[u], at(dz=-1), down)
            send(ref, ref, b_s.at[u, 3], b_r.at[u], at(dz=-2), both(plane, row0))
            for d in range(1, NX):
                needed = jnp.logical_not(jnp.logical_and(row0, (x + d) % NX == root))
                send(ref, ref, c_s.at[u, d - 1], c_r.at[u, d - 1], at(dx=d), both(plane, needed))

    def gather(chosen):
        for u, unit in chosen:
            root = unit[0] % 2
            plane = below if unit[0] < 2 else None
            needed = jnp.logical_not(pcol == root)
            for d in range(1, NX):
                ref = rows_of(unit, (x - d + NX) % NX)
                await_recv(ref, c_s.at[u, d - 1], c_r.at[u, d - 1], both(plane, needed))

    panels = [(u, unit) for u, unit in enumerate(units) if unit[0] < 2]
    corners = [(u, unit) for u, unit in enumerate(units) if unit[0] >= 2]

    scatter_parts(panels)
    spread(panels)

    for d in range(1, NY):
        part = xf.at[h, chunk((y - d + NY) % NY)]
        await_recv(part, ag_s.at[d - 1], ag_r.at[d - 1])
        send(part, part, as_s.at[d], as_r.at[d], sibling)

    def keep_corner(corner, first_row):
        corner[h] = xf[h, first_row:first_row + NB]

    pl.when(pcol == 0)(lambda: keep_corner(c10, NB))
    pl.when(pcol == 1)(lambda: keep_corner(c01, 0))
    scatter_parts(corners)
    spread(corners)

    for d in range(NY):
        part = xf.at[other, chunk((y - d + NY) % NY)]
        await_recv(part, as_s.at[d], as_r.at[d])
    for copy in factors:
        copy.wait()

    def halves(ref, rows):
        return jnp.concatenate([ref[0, rows], ref[1, rows]], axis=1)

    ur0[...] = product(l0[...], halves(xf, pl.ds(0, NB)))

    gather(panels)

    def early():
        li0[...] = product(px0[...], u0[...])
        f1[...] = xi[...] - product(li0[...], ur0[...])

    pl.when(below)(early)

    gather(corners)
    for b, corner in ((0, c10), (1, c01)):
        send(corner.at[h], corner.at[h], cs_s.at[b], cs_r.at[b], sibling)
    for b, corner in ((0, c10), (1, c01)):
        await_recv(corner.at[other], cs_s.at[b], cs_r.at[b])

    def first_block():
        @pl.when(pcol == 0)
        def _():
            out_ref[...] = halves(xf, pl.ds(0, NB))

        @pl.when(pcol > 0)
        def _():
            out_ref[...] = ur0[...]

    def other_blocks():
        whole = pl.ds(0, NB)
        lower10 = product(halves(c10, whole), u0[...])

        @pl.when(jnp.logical_and(top, pcol == 0))
        def _():
            out_ref[...] = lower10

        @pl.when(jnp.logical_not(jnp.logical_and(top, pcol == 0)))
        def _():
            second = halves(xf, pl.ds(NB, NB)) - product(lower10, ur0[...])

            @pl.when(jnp.logical_and(top, pcol == 1))
            def _():
                out_ref[...] = second

            @pl.when(jnp.logical_and(top, pcol > 1))
            def _():
                out_ref[...] = product(l1[...], second)

            @pl.when(below)
            def _():
                urow = product(l1[...], second)
                upper01 = product(l0[...], halves(c01, whole))
                lower1 = product(px1[...] - product(li0[...], upper01), u1[...])

                @pl.when(pcol == 0)
                def _():
                    out_ref[...] = li0[...]

                @pl.when(pcol == 1)
                def _():
                    out_ref[...] = lower1

                @pl.when(pcol > 1)
                def _():
                    out_ref[...] = f1[...] - product(lower1, urow)

    pl.when(prow == 0)(first_block)
    pl.when(prow > 0)(other_blocks)

    for cond, copy in pending:
        when(cond, copy.wait_send)


def on_device(
    matrix, pivots_first, pivots_second, lower_first, upper_first, lower_second, upper_second
):
    vmem = pl.BlockSpec(memory_space=pltpu.VMEM)
    anywhere = pl.BlockSpec(memory_space=pl.ANY)
    block = (NB, NB)
    dma = pltpu.SemaphoreType.DMA
    nu = 4 * SUBS
    return pl.pallas_call(
        kernel,
        out_shape=jax.ShapeDtypeStruct(block, F32),
        in_specs=[vmem] * 3 + [anywhere] * 4,
        out_specs=vmem,
        scratch_shapes=[pltpu.VMEM(block, F32)] * 4
        + [
            pltpu.VMEM((2 * NB, NB), F32),
            pltpu.VMEM((2 * NB, HALF), F32),
            pltpu.VMEM((2 * NB, HALF), F32),
            pltpu.VMEM((NY - 1, HALF, HALF), F32),
            pltpu.VMEM((2, 2 * NB, HALF), F32),
            pltpu.VMEM((2, NB, NB), F32),
            pltpu.VMEM(block, F32),
            pltpu.VMEM(block, F32),
            pltpu.VMEM(block, F32),
            pltpu.VMEM((2, NB, HALF), F32),
            pltpu.VMEM((2, NB, HALF), F32),
            pltpu.VMEM(block, F32),
            pltpu.VMEM(block, F32),
            pltpu.VMEM(block, F32),
        ]
        + [
            dma((4,)),
            dma((2,)), dma((2,)),
            dma((2, WCH)), dma((2, WCH)),
            dma((2, WCH)), dma((2, WCH)),
            dma((NY - 1,)), dma((NY - 1,)),
            dma((NY - 1,)), dma((NY - 1,)),
            dma((NY,)), dma((NY,)),
            dma((nu, NX - 1)), dma((nu,)),
            dma((nu, 4)), dma((nu,)),
            dma((nu, NX - 1)), dma((nu, NX - 1)),
            dma((2,)), dma((2,)),
        ],
        compiler_params=pltpu.CompilerParams(
            collective_id=0, has_side_effects=True, vmem_limit_bytes=56 << 20
        ),
    )(
        matrix, pivots_first.reshape(1, NB), pivots_second.reshape(1, NB),
        lower_first, upper_first, lower_second, upper_second,
    )


def solution(mesh):
    placed = (P("prow", "pcol"), P(), P(), P(), P(), P(), P())
    return jax.shard_map(
        on_device, mesh=mesh, in_specs=placed, out_specs=P("prow", "pcol"), check_vma=False
    )
```

```python
import functools

import jax
import jax.numpy as jnp
from jax import lax
from jax.experimental import pallas as pl
from jax.experimental.pallas import tpu as pltpu
from jax.sharding import PartitionSpec as P

MESH = pl.DeviceIdType.MESH
NB = 512
HALF = NB // 2
NY, NC, NZ, NX = 4, 2, 8, 4
PART = NB // NX
SUBS = 2
SUB = PART // SUBS
WCH = 4
WCOLS = NB // WCH
RCH = 8
RROWS = HALF // 2
LAG = 2
PAIRED = (0, 1, 4, 5, 8, 9)
RETURNED = (0, 1, 2, 3, 4, 5, 6, 7)
F32 = jnp.float32
BF16 = jnp.bfloat16


def dot1(a, b):
    return jnp.dot(a, b, preferred_element_type=F32)


def split2(a):
    high = a.astype(BF16)
    return high, (a - high.astype(F32)).astype(BF16)


def split3(a):
    high = a.astype(BF16)
    rest = a - high.astype(F32)
    mid = rest.astype(BF16)
    return high, mid, (rest - mid.astype(F32)).astype(BF16)


def product(a, b):
    ah, al = split2(a)
    bh, bl = split2(b)
    return dot1(ah, bh) + (dot1(ah, bl) + dot1(al, bh))


def pick(onehot, parts):
    high, mid, low = parts
    return dot1(onehot, high) + (dot1(onehot, mid) + dot1(onehot, low))


def onehot_of(source, first):
    lanes = lax.broadcasted_iota(jnp.int32, (NB, NB), 1).astype(F32) + first
    return jnp.where(source == lanes, 1.0, 0.0).astype(BF16)


def kernel(
    w_ref, pf_ref, ps_ref, l0_hbm, u0_hbm, l1_hbm, u1_hbm, out_ref,
    l0, u0, l1, u1, xp, sib, hs, turn, mb, xf, xi, px0, px1, c10, c01, ur0, f1,
    gmid, ulmid, bmid, amid, hot, own, moved, fac_sem, sib_s, sib_r,
    p1_s, p1_r, p2f_s, p2f_r, p2b_s, p2b_r, ms_s, ms_r, xs_s, xs_r,
    a_s, a_r, b_s, b_r, c_s, c_r, r_s, r_r, cs_s, cs_r, tmid,
):
    prow = lax.axis_index("prow")
    pcol = lax.axis_index("pcol")
    y, h = prow // 2, prow % 2
    z, x = pcol // NX, pcol % NX
    other = 1 - h
    top = y == 0
    below = y > 0
    row0 = z == 0
    rooted = pcol < 2
    lead = jnp.where(pcol == 0, 1, 0)

    def at(dy=0, dc=0, dz=0, dx=0):
        return {
            "prow": ((y + dy + NY) % NY) * NC + (h + dc) % NC,
            "pcol": ((z + dz + NZ) % NZ) * NX + (x + dx + NX) % NX,
        }

    sibling = at(dc=1)
    pending = []

    def both(*conds):
        conds = [c for c in conds if c is not None]
        return functools.reduce(jnp.logical_and, conds) if conds else None

    def when(cond, fn):
        if cond is None:
            fn()
        else:
            pl.when(cond)(fn)

    def remote(src, dst, ssem, rsem, device):
        return pltpu.make_async_remote_copy(
            src_ref=src, dst_ref=dst, send_sem=ssem, recv_sem=rsem, device_id=device, device_id_type=MESH
        )

    def send(src, dst, ssem, rsem, device, cond=None):
        copy = remote(src, dst, ssem, rsem, device)
        when(cond, copy.start)
        pending.append((cond, copy))

    def await_recv(dst, ssem, rsem, cond=None):
        when(cond, remote(dst, dst, ssem, rsem, sibling).wait_recv)

    factors = [
        pltpu.make_async_copy(src, dst, fac_sem.at[k])
        for k, (src, dst) in enumerate(((l0_hbm, l0), (u0_hbm, u0), (l1_hbm, l1), (u1_hbm, u1)))
    ]
    for copy in factors:
        copy.start()

    partners = [
        at(dc=1), at(dy=1), at(dy=2), at(dy=3), at(dx=1), at(dx=2), at(dx=3),
        at(dz=1), at(dz=2), at(dz=-1), at(dz=-2),
    ]
    barrier = pltpu.get_barrier_semaphore()
    for partner in partners:
        pl.semaphore_signal(barrier, inc=1, device_id=partner, device_id_type=MESH)

    base = (prow * NB).astype(F32)
    chip = (y * 2 * NB).astype(F32)
    pf_row = pf_ref[...].astype(F32)
    ps_row = ps_ref[...].astype(F32)
    row_id = lax.broadcasted_iota(jnp.int32, (NB, NB), 0).astype(F32)
    col_id = lax.broadcasted_iota(jnp.int32, (NB, NB), 1).astype(F32)
    slot_col = row_id[:, 0:1]
    diagonal = row_id == col_id
    pf_col = jnp.sum(jnp.where(diagonal, pf_row, 0.0), axis=1, keepdims=True)
    ps_col = jnp.sum(jnp.where(diagonal, ps_row, 0.0), axis=1, keepdims=True)
    chained = jnp.sum(jnp.where(ps_col == pf_row, col_id + 1.0, 0.0), axis=1, keepdims=True)
    src1 = jnp.where(chained > 0.0, chained - 1.0, ps_col)
    linked_col = jnp.sum(jnp.where(pf_row == row_id + float(NB), col_id + 1.0, 0.0), axis=1, keepdims=True)
    origin_col = jnp.where(linked_col > 0.0, linked_col - 1.0, slot_col + float(NB))
    linked_row = jnp.sum(jnp.where(pf_col == col_id + float(NB), row_id + 1.0, 0.0), axis=0, keepdims=True)
    origin_row = jnp.where(linked_row > 0.0, linked_row, col_id[0:1] + float(NB + 1))
    again = jnp.sum(jnp.where(pf_col == ps_row, origin_row, 0.0), axis=1, keepdims=True)
    back0 = jnp.where(again > 0.0, again - 1.0, slot_col)
    held = float(2 * NB)
    swap0 = jnp.where(jnp.logical_and(top, pf_col >= held), back0, pf_col)
    swap1 = jnp.where(jnp.logical_and(top, src1 >= held), origin_col, src1)
    far = pl.multiple_of(other * HALF, HALF)
    near = pl.multiple_of(h * HALF, HALF)
    wanted = [onehot_of(jnp.where(lead == stage, swap0, swap1), base) for stage in range(2)]
    w_far = split3(w_ref[:, pl.ds(far, HALF)])
    for stage in range(2):
        xp[stage] = pick(wanted[stage], w_far)

    pl.semaphore_wait(barrier, len(partners))

    for c in range(2):
        cols = pl.ds(c * WCOLS, WCOLS)
        for stage in range(2):
            sems = (sib_s.at[c, stage], sib_r.at[c, stage])
            send(xp.at[stage, :, cols], sib.at[stage, :, cols], *sems, sibling)
    w_near = split3(w_ref[:, pl.ds(near, HALF)])
    for stage in range(2):
        hs[stage] = pick(wanted[stage], w_near)

    for stage in range(2):
        source = jnp.where(lead == stage, pf_col, src1)
        inside = jnp.logical_and(source >= chip, source < chip + held)
        own[stage] = jnp.where(inside, 1.0, 0.0)

    def add_other(c):
        cols = pl.ds(c * WCOLS, WCOLS)
        for stage in range(2):
            await_recv(sib.at[stage, :, cols], sib_s.at[c, stage], sib_r.at[c, stage])
            hs[stage, :, cols] = hs[stage, :, cols] + sib[stage, :, cols]

    def piece(way, j):
        s, sub = (j // 2) % 2, j % 2
        rows = pl.ds(way * HALF + sub * RROWS, RROWS)
        cols = pl.ds((j // 4) * WCOLS, WCOLS)
        return s, rows, cols

    ring = {}
    for way in range(2):
        dy = 1 - 2 * way
        first = y == 0
        last = y == (3 if way == 0 else 1)
        between = both(below, jnp.logical_not(last))
        for j in range(RCH):
            where = piece(way, j)
            into = mb.at[(h,) + where]
            done = xf.at[(h,) + where]
            p1 = (p1_s.at[way, j], p1_r.at[way, j])
            copies = dict(
                begin=remote(hs.at[where], into, *p1, at(dy=dy)),
                onward=remote(turn.at[where], into, *p1, at(dy=dy)),
                forth=remote(done, done, p2f_s.at[way, j], p2f_r.at[way, j], at(dy=dy)),
                back=remote(done, done, p2b_s.at[way, j], p2b_r.at[way, j], at(dy=-dy)),
                raw=remote(into, into, ms_s.at[way, j], ms_r.at[way, j], sibling),
                final=remote(done, done, xs_s.at[way, j], xs_r.at[way, j], sibling),
            )
            ring[way, j] = copies
            pending.append((first, copies["begin"]))
            pending.append((between, copies["onward"]))
            pending.append((jnp.logical_or(first, last), copies["forth"]))
            pending.append((last, copies["back"]))
            pending.append((below, copies["raw"]))
            pending.append((None, copies["final"]))

    def first_pass(way, j, hop):
        copies = ring[way, j]
        where = piece(way, j)
        s, rows, cols = where
        copies["onward"].wait_recv()
        copies["raw"].start()
        merged = jnp.where(own[s, rows] > 0.0, hs[where], mb[(h,) + where])
        if hop < NY - 1:
            turn[where] = merged
            copies["onward"].start()
        else:
            xf[(h,) + where] = merged
            copies["forth"].start()
            copies["back"].start()
            copies["final"].start()

    def second_pass(way, j, hop):
        copies = ring[way, j]
        if hop == 2:
            copies["back"].wait_recv()
        else:
            copies["forth"].wait_recv()
        if hop == 0:
            copies["forth"].start()
        copies["final"].start()

    events = {}
    for v in range(NY):
        for way in range(2):
            hop = v if way == 0 else (NY - v) % NY
            for j in range(RCH):
                if hop > 0:
                    events.setdefault((LAG * hop + j, v), []).append((first_pass, way, j, hop))
                if hop < 3:
                    lag = {0: 4, 1: 5, 2: 4}[hop]
                    events.setdefault((LAG * lag + j, v), []).append((second_pass, way, j, hop))

    def slots(begin, end):
        for v in range(NY):
            todo = [e for key in range(begin, end) for e in events.get((key, v), ())]

            def run(todo=todo):
                for fn, way, j, hop in todo:
                    fn(way, j, hop)

            if todo:
                pl.when(y == v)(run)

    def begin_ring(c):
        for j in range(4 * c, 4 * c + 4):
            for way in range(2):
                ring[way, j]["begin"].start()

    def find_rows():
        src1_row = jnp.sum(jnp.where(pf_col == ps_row, row_id + 1.0, 0.0), axis=0, keepdims=True)
        src1_row = jnp.where(src1_row > 0.0, src1_row - 1.0, ps_row)
        count = jnp.zeros((NB, 1), F32)
        for stage in range(2):
            source = jnp.where(lead == stage, pf_row, src1_row)
            mark = jnp.where(source == base + row_id, 1.0, 0.0)
            hot[stage] = mark.astype(BF16)
            count += jnp.sum(mark, axis=1, keepdims=True)
        moved[...] = count

    def place(c):
        for way in range(2):
            for j in range(4 * c, 4 * c + 4):
                ref = mb.at[(other,) + piece(way, j)]
                await_recv(ref, ms_s.at[way, j], ms_r.at[way, j])
        cols = pl.ds(c * WCOLS, WCOLS)
        incoming = jnp.zeros((NB, 2 * WCOLS), F32)
        for stage in range(2):
            rows = jnp.concatenate([mb[0, stage, :, cols], mb[1, stage, :, cols]], axis=1)
            incoming += pick(hot[stage], split3(rows))
        for side in range(2):
            there = pl.ds(side * HALF + c * WCOLS, WCOLS)
            placed = jnp.where(moved[...] > 0.0, incoming[:, side * WCOLS:(side + 1) * WCOLS], w_ref[:, there])
            xi[:, there] = placed

    def place_panel(c):
        @pl.when(both(below, rooted))
        def _():
            place(c)
            for side in range(2):
                there = pl.ds(side * HALF + c * WCOLS, WCOLS)

                @pl.when(pcol == 0)
                def _():
                    px0[:, there] = xi[:, there]

                @pl.when(pcol == 1)
                def _():
                    px1[:, there] = xi[:, there]

    def place_rest(c):
        pl.when(both(below, jnp.logical_not(rooted)))(lambda: place(c))

    def collect_other(stage):
        for way in range(2):
            for j in range(RCH):
                if piece(way, j)[0] == stage:
                    ref = xf.at[(other,) + piece(way, j)]
                    await_recv(ref, xs_s.at[way, j], xs_r.at[way, j])

    units = [(b, s) for s in (0, 2, 1, 3) for b in range(2)] + [(b, s) for b in (2, 3) for s in range(SUBS)]

    def rows_of(unit, part, half=None):
        b, sub = unit
        count = PART if b < 2 else SUB
        first = part * PART + (0 if b < 2 else sub * SUB)
        if half is not None:
            count = count // 2
            first = first + half * count
        rows = pl.ds(pl.multiple_of(first, count), count)
        if b < 2:
            return (px0, px1)[b].at[rows, pl.ds(sub * WCOLS, WCOLS)]
        return (c10, c01)[b - 2].at[h, rows]

    def parts_of(u, column):
        return (column % NX, (column + 2) % NX) if u in PAIRED else (column % NX,)

    def unit_steps(u):
        unit = units[u]
        root = unit[0] % 2
        shared = unit[0] >= 2
        first, later, last = [], [], []

        def put(steps, src, ssem, rsem, device, cond):
            copy = remote(src, src, ssem, rsem, device)
            steps.append((cond, copy.start))
            pending.append((both(None if shared else below, cond), copy))

        def take(steps, ref, ssem, rsem, cond):
            steps.append((cond, remote(ref, ref, ssem, rsem, sibling).wait_recv))

        def across(steps, part, slot):
            ref = rows_of(unit, part)
            sems = (unit[0] - 2, unit[1], slot)
            put(steps, ref, cs_s.at[sems], cs_r.at[sems], sibling, None)

        for d in (1, 3, 2):
            for slot, part in enumerate(parts_of(u, root + d)):
                put(first, rows_of(unit, part), a_s.at[u, slot, d - 1], a_r.at[u, slot], at(dx=d), pcol == root)

        forks = jnp.logical_or(z == 2, z == 6)
        for slot, part in enumerate(parts_of(u, x)):
            ref = rows_of(unit, part)
            take(later, ref, a_s.at[u, slot, 0], a_r.at[u, slot], both(row0, x != root))
            take(later, ref, b_s.at[u, slot, 0], b_r.at[u, slot], z != 0)
            for k, (dz, cond) in enumerate((
                (2, row0), (-2, row0), (1, jnp.logical_or(forks, z == 3)), (-1, forks),
            )):
                put(later, ref, b_s.at[u, slot, k], b_r.at[u, slot], at(dz=dz), cond)
        ref = rows_of(unit, x)
        for d in (1, 3) if u in PAIRED else (1, 3, 2):
            away = z != 0 if u in RETURNED else jnp.logical_not(both(row0, (x + d) % NX == root))
            put(later, ref, c_s.at[u, d - 1], c_r.at[u, d - 1], at(dx=d), away)
        if shared:
            for slot, part in enumerate(parts_of(u, x)):
                across(later, part, 2 * slot)

        for d in (1, 3) if u in PAIRED else (1, 3, 2):
            part = (x + d) % NX
            take(last, rows_of(unit, part), c_s.at[u, 3 - d], c_r.at[u, 3 - d], z != 0 if u in RETURNED else pcol != root)
            pieces = {1: ((None, 1, 0),), 3: ((None, 7, 1),), 2: ((0, 1, 2), (1, 7, 3))}[d]
            for half, level, slot in pieces if u in RETURNED else ():
                ref = rows_of(unit, part, half)
                dz = 1 if level == 7 else -1
                put(last, ref, r_s.at[u, slot], r_r.at[u, slot], at(dz=dz), both(z == level, x != root))
                take(last, ref, r_s.at[u, slot], r_r.at[u, slot], both(row0, x != root))
            if shared:
                across(last, part, d)
        return first, later, last

    steps_of = [unit_steps(u) for u in range(2 * WCH + 2 * SUBS)]

    def carry(phase, chosen, role=None):
        for wanted, plane in ((lambda u: units[u][0] < 2, below), (lambda u: units[u][0] >= 2, None)):
            group = [u for u in chosen if wanted(u)]

            def run(group=group):
                for u in group:
                    for cond, act in steps_of[u][phase]:
                        when(cond, act)

            if group:
                when(both(plane, role), run)

    scatter = functools.partial(carry, 0)
    spread = functools.partial(carry, 1)
    gather = functools.partial(carry, 2)
    is_root = both(row0, rooted)
    is_entry = both(row0, jnp.logical_not(rooted))
    is_fork = jnp.logical_or(z == 2, z == 6)
    is_edge = jnp.logical_or(z == 1, z == 7)
    is_inner = jnp.logical_not(is_edge)
    is_leaf = both(z != 0, jnp.logical_not(is_fork))
    is_far = z != 0

    def spread_own(chosen, mine):
        for column in range(2):
            spread([u for u in chosen if (units[u][0] % 2 == column) == mine], both(row0, pcol == column))

    panel = (tuple(range(0, 4)), tuple(range(4, 8)))
    corner10 = tuple(range(2 * WCH, 2 * WCH + SUBS))
    corner01 = tuple(range(2 * WCH + SUBS, 2 * WCH + 2 * SUBS))
    corners = corner10 + corner01

    def keep_corner(corner):
        corner[h] = xf[h, 0]

    def pivot_rows(q):
        stage = jnp.where(lead == 1, 1 - q, q)
        return jnp.concatenate([xf[0, stage], xf[1, stage]], axis=1)

    for c in range(2):
        add_other(c)
        pl.when(top)(functools.partial(begin_ring, c))
    slots(0, 4)
    pl.when(below)(find_rows)
    slots(4, 6)
    for copy in factors:
        copy.wait()

    @pl.when(below)
    def _():
        gmid[...] = product(u1[...], l1[...])
        ulmid[...] = product(u0[...], l0[...])

    slots(6, 10)
    place_panel(0)
    scatter(panel[0], is_root)
    spread_own(panel[0], True)
    spread(panel[0], is_entry)
    slots(10, 14)
    spread_own(panel[0], False)
    place_panel(1)
    scatter(panel[1], is_root)
    spread_own(panel[1], True)
    spread(panel[0], is_fork)
    slots(14, 16)
    pl.when(pcol == 0)(lambda: keep_corner(c10))
    pl.when(pcol == 1)(lambda: keep_corner(c01))
    scatter(corners, is_root)
    spread_own(corners, True)
    spread_own(panel[1], False)
    spread(panel[1], is_entry)
    spread(panel[0], is_leaf)
    spread_own(corners, False)
    spread(corners, is_entry)
    spread(panel[1], is_fork)
    slots(16, 18)
    place_rest(0)
    spread(panel[1], is_leaf)
    gather(panel[0], is_edge)
    place_rest(1)
    gather(panel[1], is_edge)
    spread(corner10, is_far)
    collect_other(0)

    @pl.when(pcol > 0)
    def _():
        ur0[...] = product(l0[...], pivot_rows(0))

    spread(corner01, is_far)

    @pl.when(pcol > 0)
    def _():
        amid[...] = product(u0[...], ur0[...])

    gather(corners, is_edge)
    gather(panel[0] + panel[1], is_inner)
    def early():
        @pl.when(pcol > 0)
        def _():
            bmid[...] = product(px0[...], ulmid[...])

        @pl.when(pcol > 1)
        def _():
            f1[...] = xi[...] - product(px0[...], amid[...])

    pl.when(below)(early)
    gather(corners, is_inner)

    def whole(ref):
        return jnp.concatenate([ref[0], ref[1]], axis=1)

    def corner_other(b):
        for s in range(SUBS):
            for d in range(NX):
                rows = pl.ds(pl.multiple_of(((x + d) % NX) * PART + s * SUB, SUB), SUB)
                await_recv((c10, c01)[b].at[other, rows], cs_s.at[b, s, d], cs_r.at[b, s, d])

    collect_other(1)
    corner_other(0)

    @pl.when(both(prow > 0, pcol > 0))
    def _():
        right = pivot_rows(1) - product(whole(c10), amid[...])
        tmid[...] = right

        @pl.when(both(below, pcol > 1))
        def _():
            tmid[...] = product(gmid[...], right)

    corner_other(1)
    def first_block():
        @pl.when(pcol == 0)
        def _():
            out_ref[...] = pivot_rows(0)

        @pl.when(pcol > 0)
        def _():
            out_ref[...] = ur0[...]

    def second_block():
        @pl.when(pcol == 0)
        def _():
            out_ref[...] = product(whole(c10), u0[...])

        @pl.when(pcol > 0)
        def _():
            @pl.when(pcol == 1)
            def _():
                out_ref[...] = tmid[...]

            @pl.when(pcol > 1)
            def _():
                out_ref[...] = product(l1[...], tmid[...])

    def trailing():
        @pl.when(pcol == 0)
        def _():
            out_ref[...] = product(px0[...], u0[...])

        @pl.when(pcol > 0)
        def _():
            left = px1[...] - product(bmid[...], whole(c01))

            @pl.when(pcol == 1)
            def _():
                out_ref[...] = product(left, u1[...])

            @pl.when(pcol > 1)
            def _():
                out_ref[...] = f1[...] - product(left, tmid[...])

    pl.when(prow == 0)(first_block)
    pl.when(prow == 1)(second_block)
    pl.when(below)(trailing)

    for cond, copy in pending:
        when(cond, copy.wait_send)


def on_device(
    matrix, pivots_first, pivots_second, lower_first, upper_first, lower_second, upper_second
):
    vmem = pl.BlockSpec(memory_space=pltpu.VMEM)
    anywhere = pl.BlockSpec(memory_space=pl.ANY)
    block = (NB, NB)
    dma = pltpu.SemaphoreType.DMA
    nu = 2 * WCH + 2 * SUBS
    return pl.pallas_call(
        kernel,
        out_shape=jax.ShapeDtypeStruct(block, F32),
        in_specs=[vmem] * 3 + [anywhere] * 4,
        out_specs=vmem,
        scratch_shapes=[pltpu.VMEM(block, F32)] * 4
        + [
            pltpu.VMEM((2, NB, HALF), F32),
            pltpu.VMEM((2, NB, HALF), F32),
            pltpu.VMEM((2, NB, HALF), F32),
            pltpu.VMEM((2, NB, HALF), F32),
            pltpu.VMEM((2, 2, NB, HALF), F32),
            pltpu.VMEM((2, 2, NB, HALF), F32),
            pltpu.VMEM(block, F32),
            pltpu.VMEM(block, F32),
            pltpu.VMEM(block, F32),
            pltpu.VMEM((2, NB, HALF), F32),
            pltpu.VMEM((2, NB, HALF), F32),
        ]
        + [pltpu.VMEM(block, F32)] * 6
        + [pltpu.VMEM((2, NB, NB), BF16), pltpu.VMEM((2, NB, 1), F32), pltpu.VMEM((NB, 1), F32)]
        + [dma((4,)), dma((2, 2)), dma((2, 2))]
        + [dma((2, RCH))] * 10
        + [
            dma((nu, 2, NX - 1)), dma((nu, 2)),
            dma((nu, 2, 4)), dma((nu, 2)),
            dma((nu, NX - 1)), dma((nu, NX - 1)),
            dma((nu, 4)), dma((nu, 4)),
            dma((2, SUBS, NX)), dma((2, SUBS, NX)),
            pltpu.VMEM(block, F32),
        ],
        compiler_params=pltpu.CompilerParams(
            collective_id=0, has_side_effects=True, vmem_limit_bytes=56 << 20
        ),
    )(
        matrix, pivots_first.reshape(1, NB), pivots_second.reshape(1, NB),
        lower_first, upper_first, lower_second, upper_second,
    )


def solution(mesh):
    placed = (P("prow", "pcol"), P(), P(), P(), P(), P(), P())
    return jax.shard_map(
        on_device, mesh=mesh, in_specs=placed, out_specs=P("prow", "pcol"), check_vma=False
    )
```

```python
import functools

import jax
import jax.numpy as jnp
from jax import lax
from jax.experimental import pallas as pl
from jax.experimental.pallas import tpu as pltpu
from jax.sharding import PartitionSpec as P

MESH = pl.DeviceIdType.MESH
NB = 512
HALF = NB // 2
NY, NC, NZ, NX = 4, 2, 8, 4
PART = NB // NX
SUBS = 2
SUB = PART // SUBS
WCH = 4
WCOLS = NB // WCH
RCH = 8
RROWS = HALF // 2
LAG = 2
PAIRED = (2, 3, 4, 5, 8, 9, 10, 11)
RETURNED = (0, 1, 2, 3)
F32 = jnp.float32
BF16 = jnp.bfloat16


def dot1(a, b):
    return jnp.dot(a, b, preferred_element_type=F32)


def split2(a):
    high = a.astype(BF16)
    return high, (a - high.astype(F32)).astype(BF16)


def split3(a):
    high = a.astype(BF16)
    rest = a - high.astype(F32)
    mid = rest.astype(BF16)
    return high, mid, (rest - mid.astype(F32)).astype(BF16)


def product(a, b):
    ah, al = split2(a)
    bh, bl = split2(b)
    return dot1(ah, bh) + (dot1(ah, bl) + dot1(al, bh))


def pick(onehot, parts):
    high, mid, low = parts
    return dot1(onehot, high) + (dot1(onehot, mid) + dot1(onehot, low))


def onehot_of(source, first):
    lanes = lax.broadcasted_iota(jnp.int32, (NB, NB), 1).astype(F32) + first
    return jnp.where(source == lanes, 1.0, 0.0).astype(BF16)


def kernel(
    w_ref, pf_ref, ps_ref, l0_hbm, u0_hbm, l1_hbm, u1_hbm, out_ref,
    l0, u0, l1, u1, xp, sib, hs, turn, mb, xf, xi, px0, px1, c10, c01, ur0, f1,
    gmid, ulmid, bmid, amid, hot, own, moved, fac_sem, sib_s, sib_r,
    p1_s, p1_r, p2f_s, p2f_r, p2b_s, p2b_r, ms_s, ms_r, xs_s, xs_r,
    a_s, a_r, b_s, b_r, c_s, c_r, r_s, r_r, y_s, y_r, cs_s, cs_r, tmid, left_near,
):
    prow = lax.axis_index("prow")
    pcol = lax.axis_index("pcol")
    y, h = prow // 2, prow % 2
    z, x = pcol // NX, pcol % NX
    other = 1 - h
    top = y == 0
    below = y > 0
    row0 = z == 0
    rooted = pcol < 2
    lead = jnp.where(pcol == 0, 1, 0)

    def at(dy=0, dc=0, dz=0, dx=0):
        return {
            "prow": ((y + dy + NY) % NY) * NC + (h + dc) % NC,
            "pcol": ((z + dz + NZ) % NZ) * NX + (x + dx + NX) % NX,
        }

    sibling = at(dc=1)
    pending = []

    def both(*conds):
        conds = [c for c in conds if c is not None]
        return functools.reduce(jnp.logical_and, conds) if conds else None

    def when(cond, fn):
        if cond is None:
            fn()
        else:
            pl.when(cond)(fn)

    def drain():
        groups = {}
        for cond, copy in pending:
            groups.setdefault(id(cond), (cond, []))[1].append(copy)
        pending.clear()
        for cond, copies in groups.values():

            def run(copies=copies):
                for copy in copies:
                    copy.wait_send()

            when(cond, run)

    known = {}

    def named(name, make):
        if name not in known:
            known[name] = make()
        return known[name]

    def remote(src, dst, ssem, rsem, device):
        return pltpu.make_async_remote_copy(
            src_ref=src, dst_ref=dst, send_sem=ssem, recv_sem=rsem, device_id=device, device_id_type=MESH
        )

    def send(src, dst, ssem, rsem, device, cond=None):
        copy = remote(src, dst, ssem, rsem, device)
        when(cond, copy.start)
        pending.append((cond, copy))

    def await_recv(dst, ssem, rsem, cond=None):
        when(cond, remote(dst, dst, ssem, rsem, sibling).wait_recv)

    factors = [
        pltpu.make_async_copy(src, dst, fac_sem.at[k])
        for k, (src, dst) in enumerate(((l0_hbm, l0), (u0_hbm, u0), (l1_hbm, l1), (u1_hbm, u1)))
    ]
    for copy in factors:
        copy.start()

    ahead = both(row0, rooted)
    later = jnp.logical_not(ahead)
    column = [at(dc=1), at(dy=1), at(dy=2), at(dy=3)]
    moves = [(0, 1), (0, 2), (0, 3), (1, 0), (2, 0), (-1, 0), (-2, 0)]
    crosswise = []
    for dz, dx in moves:
        theirs = both((z + dz + NZ) % NZ == 0, (x + dx) % NX < 2)
        crosswise.append((at(dz=dz, dx=dx), theirs))
    barrier = pltpu.get_barrier_semaphore()

    def greet(device):
        pl.semaphore_signal(barrier, inc=1, device_id=device, device_id_type=MESH)

    for device in column:
        greet(device)
    for device, theirs in crosswise:
        pl.when(ahead == theirs)(functools.partial(greet, device))

    base = (prow * NB).astype(F32)
    chip = (y * 2 * NB).astype(F32)
    pf_row = pf_ref[...].astype(F32)
    ps_row = ps_ref[...].astype(F32)
    row_id = lax.broadcasted_iota(jnp.int32, (NB, NB), 0).astype(F32)
    col_id = lax.broadcasted_iota(jnp.int32, (NB, NB), 1).astype(F32)
    slot_col = row_id[:, 0:1]
    diagonal = row_id == col_id
    pf_col = jnp.sum(jnp.where(diagonal, pf_row, 0.0), axis=1, keepdims=True)
    ps_col = jnp.sum(jnp.where(diagonal, ps_row, 0.0), axis=1, keepdims=True)
    chained = jnp.sum(jnp.where(ps_col == pf_row, col_id + 1.0, 0.0), axis=1, keepdims=True)
    src1 = jnp.where(chained > 0.0, chained - 1.0, ps_col)
    linked_col = jnp.sum(jnp.where(pf_row == row_id + float(NB), col_id + 1.0, 0.0), axis=1, keepdims=True)
    origin_col = jnp.where(linked_col > 0.0, linked_col - 1.0, slot_col + float(NB))
    linked_row = jnp.sum(jnp.where(pf_col == col_id + float(NB), row_id + 1.0, 0.0), axis=0, keepdims=True)
    origin_row = jnp.where(linked_row > 0.0, linked_row, col_id[0:1] + float(NB + 1))
    again = jnp.sum(jnp.where(pf_col == ps_row, origin_row, 0.0), axis=1, keepdims=True)
    back0 = jnp.where(again > 0.0, again - 1.0, slot_col)
    held = float(2 * NB)
    swap0 = jnp.where(jnp.logical_and(top, pf_col >= held), back0, pf_col)
    swap1 = jnp.where(jnp.logical_and(top, src1 >= held), origin_col, src1)
    far = pl.multiple_of(other * HALF, HALF)
    near = pl.multiple_of(h * HALF, HALF)
    wanted = [onehot_of(jnp.where(lead == stage, swap0, swap1), base) for stage in range(2)]
    w_far = split3(w_ref[:, pl.ds(far, HALF)])
    for stage in range(2):
        xp[stage] = pick(wanted[stage], w_far)

    @pl.when(ahead)
    def _():
        pl.semaphore_wait(barrier, len(column) + 1)
        for device, theirs in crosswise:
            pl.when(jnp.logical_not(theirs))(functools.partial(greet, device))

    @pl.when(later)
    def _():
        pl.semaphore_wait(barrier, len(column) + len(crosswise))
        for device, theirs in crosswise:
            pl.when(theirs)(functools.partial(greet, device))


    for c in range(2):
        cols = pl.ds(c * WCOLS, WCOLS)
        for stage in range(2):
            sems = (sib_s.at[c, stage], sib_r.at[c, stage])
            send(xp.at[stage, :, cols], sib.at[stage, :, cols], *sems, sibling)
    w_near = split3(w_ref[:, pl.ds(near, HALF)])
    for stage in range(2):
        hs[stage] = pick(wanted[stage], w_near)

    for stage in range(2):
        source = jnp.where(lead == stage, pf_col, src1)
        inside = jnp.logical_and(source >= chip, source < chip + held)
        own[stage] = jnp.where(inside, 1.0, 0.0)

    def add_other(c):
        cols = pl.ds(c * WCOLS, WCOLS)
        for stage in range(2):
            await_recv(sib.at[stage, :, cols], sib_s.at[c, stage], sib_r.at[c, stage])
            hs[stage, :, cols] = hs[stage, :, cols] + sib[stage, :, cols]

    def piece(way, j):
        s, sub = (j // 2) % 2, j % 2
        rows = pl.ds(way * HALF + sub * RROWS, RROWS)
        cols = pl.ds((j // 4) * WCOLS, WCOLS)
        return s, rows, cols

    ring = {}
    for way in range(2):
        dy = 1 - 2 * way
        first = y == 0
        last = y == (3 if way == 0 else 1)
        between = both(below, jnp.logical_not(last))
        whole_ring = jnp.logical_not(rooted)
        forth_cond = jnp.logical_or(last, both(first, whole_ring))
        back_cond = both(last, whole_ring)
        final_cond = jnp.logical_or(top, whole_ring)
        for j in range(RCH):
            where = piece(way, j)
            into = mb.at[(h,) + where]
            done = xf.at[(h,) + where]
            p1 = (p1_s.at[way, j], p1_r.at[way, j])
            copies = dict(
                begin=remote(hs.at[where], into, *p1, at(dy=dy)),
                onward=remote(turn.at[where], into, *p1, at(dy=dy)),
                forth=remote(done, done, p2f_s.at[way, j], p2f_r.at[way, j], at(dy=dy)),
                back=remote(done, done, p2b_s.at[way, j], p2b_r.at[way, j], at(dy=-dy)),
                raw=remote(into, into, ms_s.at[way, j], ms_r.at[way, j], sibling),
                final=remote(done, done, xs_s.at[way, j], xs_r.at[way, j], sibling),
            )
            ring[way, j] = copies
            pending.append((first, copies["begin"]))
            pending.append((between, copies["onward"]))
            pending.append((forth_cond, copies["forth"]))
            pending.append((back_cond, copies["back"]))
            pending.append((below, copies["raw"]))
            pending.append((final_cond, copies["final"]))

    def first_pass(way, j, hop):
        copies = ring[way, j]
        where = piece(way, j)
        s, rows, cols = where
        copies["onward"].wait_recv()
        copies["raw"].start()
        merged = jnp.where(own[s, rows] > 0.0, hs[where], mb[(h,) + where])
        if hop < NY - 1:
            turn[where] = merged
            copies["onward"].start()
        else:
            xf[(h,) + where] = merged
            copies["forth"].start()

            def others():
                copies["back"].start()
                copies["final"].start()

            pl.when(jnp.logical_not(rooted))(others)

    def second_pass(way, j, hop):
        copies = ring[way, j]
        spread_on = jnp.logical_not(rooted)
        if hop == 0:
            copies["forth"].wait_recv()
            when(spread_on, copies["forth"].start)
            copies["final"].start()
        else:

            def arrive():
                copies["back" if hop == 2 else "forth"].wait_recv()
                copies["final"].start()

            when(spread_on, arrive)

    events = {}
    for v in range(NY):
        for way in range(2):
            hop = v if way == 0 else (NY - v) % NY
            for j in range(RCH):
                if hop > 0:
                    events.setdefault((LAG * hop + j, v), []).append((first_pass, way, j, hop))
                if hop < 3:
                    lag = {0: 4, 1: 5, 2: 4}[hop]
                    events.setdefault((LAG * lag + j, v), []).append((second_pass, way, j, hop))

    def slots(begin, end):
        for v in range(NY):
            todo = [e for key in range(begin, end) for e in events.get((key, v), ())]

            def run(todo=todo):
                for fn, way, j, hop in todo:
                    fn(way, j, hop)

            if todo:
                pl.when(y == v)(run)

    def begin_ring(c):
        for j in range(4 * c, 4 * c + 4):
            for way in range(2):
                ring[way, j]["begin"].start()

    def find_rows():
        src1_row = jnp.sum(jnp.where(pf_col == ps_row, row_id + 1.0, 0.0), axis=0, keepdims=True)
        src1_row = jnp.where(src1_row > 0.0, src1_row - 1.0, ps_row)
        count = jnp.zeros((NB, 1), F32)
        for stage in range(2):
            source = jnp.where(lead == stage, pf_row, src1_row)
            mark = jnp.where(source == base + row_id, 1.0, 0.0)
            hot[stage] = mark.astype(BF16)
            count += jnp.sum(mark, axis=1, keepdims=True)
        moved[...] = count

    def place(c):
        for way in range(2):
            for j in range(4 * c, 4 * c + 4):
                ref = mb.at[(other,) + piece(way, j)]
                await_recv(ref, ms_s.at[way, j], ms_r.at[way, j])
        cols = pl.ds(c * WCOLS, WCOLS)
        incoming = jnp.zeros((NB, 2 * WCOLS), F32)
        for stage in range(2):
            rows = jnp.concatenate([mb[0, stage, :, cols], mb[1, stage, :, cols]], axis=1)
            incoming += pick(hot[stage], split3(rows))
        for side in range(2):
            there = pl.ds(side * HALF + c * WCOLS, WCOLS)
            placed = jnp.where(moved[...] > 0.0, incoming[:, side * WCOLS:(side + 1) * WCOLS], w_ref[:, there])
            xi[:, there] = placed

    def place_panel(c):
        @pl.when(both(below, rooted))
        def _():
            place(c)
            for side in range(2):
                there = pl.ds(side * HALF + c * WCOLS, WCOLS)

                @pl.when(pcol == 0)
                def _():
                    px0[:, there] = xi[:, there]

                @pl.when(pcol == 1)
                def _():
                    px1[:, there] = xi[:, there]

    def place_rest(c):
        pl.when(both(below, jnp.logical_not(rooted)))(lambda: place(c))

    def collect_other(stage):
        for way in range(2):
            for j in range(RCH):
                if piece(way, j)[0] == stage:
                    ref = xf.at[(other,) + piece(way, j)]
                    await_recv(ref, xs_s.at[way, j], xs_r.at[way, j])

    units = [(b, s) for s in (0, 2, 1, 3) for b in range(2)] + [(b, s) for b in (2, 3) for s in range(SUBS)]

    corner10 = tuple(range(2 * WCH, 2 * WCH + SUBS))
    corner01 = tuple(range(2 * WCH + SUBS, 2 * WCH + 2 * SUBS))
    corners = corner10 + corner01

    def rows_of(unit, part, half=None):
        b, sub = unit
        count = PART if b < 2 else SUB
        first = part * PART + (0 if b < 2 else sub * SUB)
        if half is not None:
            count = count // 2
            first = first + half * count
        rows = pl.ds(pl.multiple_of(first, count), count)
        if b < 2:
            return (px0, px1)[b].at[rows, pl.ds(sub * WCOLS, WCOLS)]
        return (c10, c01)[b - 2].at[h, rows]

    def parts_of(u, column):
        return (column % NX, (column + 2) % NX) if u in PAIRED else (column % NX,)

    tests = {
        None: None, "row0": row0, "far": z != 0, "forks": jnp.logical_or(z == 2, z == 6),
        "rise": jnp.logical_or(jnp.logical_or(z == 2, z == 6), z == 3),
    }
    for root in range(2):
        tests["root", root] = pcol == root
        tests["apart", root] = pcol != root
        tests["enter", root] = both(row0, x != root)
        for level in (1, 7):
            tests["edge", root, level] = both(z == level, x != root)
        for d in range(1, NX):
            tests["away", root, d] = jnp.logical_not(both(row0, (x + d) % NX == root))

    def unit_steps(u):
        unit = units[u]
        root = unit[0] % 2
        shared = unit[0] >= 2
        first, later, last = [], [], []

        def put(steps, src, ssem, rsem, device, cond):
            copy = remote(src, src, ssem, rsem, device)
            steps.append((cond, copy.start))
            whole = named((shared, cond), lambda: both(top if shared else below, tests[cond]))
            pending.append((whole, copy))

        def take(steps, ref, ssem, rsem, cond):
            steps.append((cond, remote(ref, ref, ssem, rsem, sibling).wait_recv))

        def across(steps, part, slot):
            ref = rows_of(unit, part)
            sems = (unit[0] - 2, unit[1], slot)
            put(steps, ref, cs_s.at[sems], cs_r.at[sems], sibling, None)
            put(steps, ref, y_s.at[sems], y_r.at[sems], at(dy=1 if slot < 2 else -1), None)

        for d in (1, 3, 2):
            for slot, part in enumerate(parts_of(u, root + d)):
                put(first, rows_of(unit, part), a_s.at[u, slot, d - 1], a_r.at[u, slot], at(dx=d), ("root", root))

        for slot, part in enumerate(parts_of(u, x)):
            ref = rows_of(unit, part)
            take(later, ref, a_s.at[u, slot, 0], a_r.at[u, slot], ("enter", root))
            take(later, ref, b_s.at[u, slot, 0], b_r.at[u, slot], "far")
            for k, (dz, cond) in enumerate((
                (2, "row0"), (-2, "row0"), (1, "rise"), (-1, "forks"),
            )):
                put(later, ref, b_s.at[u, slot, k], b_r.at[u, slot], at(dz=dz), cond)
        ref = rows_of(unit, x)
        for d in (1, 3) if u in PAIRED else (1, 3, 2):
            away = "far" if u in RETURNED else ("away", root, d)
            put(later, ref, c_s.at[u, d - 1], c_r.at[u, d - 1], at(dx=d), away)
        if shared:
            for slot, part in enumerate(parts_of(u, x)):
                across(later, part, 2 * slot)

        for d in (1, 3) if u in PAIRED else (1, 3, 2):
            part = (x + d) % NX
            take(last, rows_of(unit, part), c_s.at[u, 3 - d], c_r.at[u, 3 - d], "far" if u in RETURNED else ("apart", root))
            pieces = {1: ((None, 1, 0),), 3: ((None, 7, 1),), 2: ((0, 1, 2), (1, 7, 3))}[d]
            for half, level, slot in pieces if u in RETURNED else ():
                ref = rows_of(unit, part, half)
                dz = 1 if level == 7 else -1
                put(last, ref, r_s.at[u, slot], r_r.at[u, slot], at(dz=dz), ("edge", root, level))
                take(last, ref, r_s.at[u, slot], r_r.at[u, slot], ("enter", root))
            if shared:
                across(last, part, d)
        return first, later, last

    steps_of = [unit_steps(u) for u in range(2 * WCH + 2 * SUBS)]

    def carry(phase, chosen, role=None):
        for wanted, plane in ((lambda u: units[u][0] < 2, below), (lambda u: units[u][0] >= 2, top)):
            group = [u for u in chosen if wanted(u)]

            def run(group=group):
                merged = []
                for u in group:
                    for cond, act in steps_of[u][phase]:
                        if merged and merged[-1][0] == cond:
                            merged[-1][1].append(act)
                        else:
                            merged.append((cond, [act]))
                for cond, acts in merged:
                    when(tests[cond], lambda acts=acts: [act() for act in acts] and None)

            if group:
                when(both(plane, role), run)

    scatter = functools.partial(carry, 0)
    spread = functools.partial(carry, 1)
    gather = functools.partial(carry, 2)
    is_root = both(row0, rooted)
    is_entry = both(row0, jnp.logical_not(rooted))
    is_fork = jnp.logical_or(z == 2, z == 6)
    is_edge = jnp.logical_or(z == 1, z == 7)
    is_inner = jnp.logical_not(is_edge)
    is_leaf = both(z != 0, jnp.logical_not(is_fork))
    is_far = z != 0

    handed = {}
    late = []
    for u in corners:
        b, s = units[u][0] - 2, units[u][1]
        for slot in range(NX):
            ref = rows_of(units[u], (x + slot) % NX)
            sems = (b, s, slot)
            onward = remote(ref, ref, y_s.at[sems], y_r.at[sems], at(dy=1 if slot < 2 else -1))
            across = remote(ref, ref, cs_s.at[sems], cs_r.at[sems], sibling)
            handed[u, slot] = onward, across
            middle = named(("middle", slot < 2), lambda: jnp.logical_or(y == 2, y == (1 if slot < 2 else 3)))
            late.append((middle, onward))
            late.append((below, across))

    def hand_down(stage):
        for v in range(1, NY):
            near, away = ((2, 3), (0, 1)) if v == 3 else ((0, 1), (2, 3))
            if v == 2:
                todo = (
                    [(u, slot) for u in corners for slot in (0, 2)],
                    [(u, slot) for u in corners for slot in (1, 3)],
                    [],
                )[stage]
            else:
                todo = (
                    [(u, near[0]) for u in corners],
                    [(u, near[1]) for u in corners],
                    [(u, slot) for slot in away for u in corners],
                )[stage]

            def run(todo=todo, v=v):
                for u, slot in todo:
                    onward, across = handed[u, slot]
                    onward.wait_recv()
                    if v == 2 or v == (1 if slot < 2 else 3):
                        onward.start()
                    across.start()

            if todo:
                pl.when(y == v)(run)

    def spread_own(chosen, mine):
        for column in range(2):
            spread([u for u in chosen if (units[u][0] % 2 == column) == mine], both(row0, pcol == column))

    panel = (tuple(range(0, 4)), tuple(range(4, 8)))

    def keep_corner(corner):
        corner[h] = xf[h, 0]

    def pivot_rows(q):
        stage = jnp.where(lead == 1, 1 - q, q)
        return jnp.concatenate([xf[0, stage], xf[1, stage]], axis=1)

    for c in range(2):
        add_other(c)
        pl.when(top)(functools.partial(begin_ring, c))
    slots(0, 4)
    pl.when(below)(find_rows)
    slots(4, 6)
    for copy in factors:
        copy.wait()

    @pl.when(below)
    def _():
        gmid[...] = product(u1[...], l1[...])
        ulmid[...] = product(u0[...], l0[...])

    slots(6, 10)
    place_panel(0)
    pl.when(ahead)(lambda: pl.semaphore_wait(barrier, len(crosswise) - 1))
    scatter(panel[0], is_root)
    spread_own(panel[0], True)
    spread(panel[0], is_entry)
    slots(10, 14)
    spread_own(panel[0], False)
    place_panel(1)
    scatter(panel[1], is_root)
    spread_own(panel[1], True)
    spread(panel[0], is_fork)
    slots(14, 16)
    pl.when(both(top, pcol == 0))(lambda: keep_corner(c10))
    pl.when(both(top, pcol == 1))(lambda: keep_corner(c01))
    scatter(corners, is_root)
    spread_own(corners, True)
    spread_own(panel[1], False)
    spread(panel[1], is_entry)
    spread(panel[0], is_leaf)
    spread_own(corners, False)
    spread(corners, is_entry)
    spread(panel[1], is_fork)
    slots(16, 18)
    place_rest(0)
    spread(panel[1], is_leaf)
    spread(corner10, is_far)
    spread(corner01, is_far)
    gather(corner10)
    gather(corner01)
    gather(panel[0], is_edge)
    place_rest(1)
    hand_down(0)
    hand_down(1)
    apart = jnp.logical_or(top, jnp.logical_not(rooted))
    pl.when(apart)(lambda: collect_other(0))

    @pl.when(both(pcol > 0, apart))
    def _():
        ur0[...] = product(l0[...], pivot_rows(0))
        amid[...] = product(u0[...], ur0[...])

    gather(panel[0], is_inner)
    gather(panel[1])
    def early():
        @pl.when(pcol > 0)
        def _():
            bmid[...] = product(px0[...], ulmid[...])

        @pl.when(pcol > 1)
        def _():
            f1[...] = xi[...] - product(px0[...], amid[...])

    pl.when(below)(early)
    drain()
    hand_down(2)

    def whole(ref):
        return jnp.concatenate([ref[0], ref[1]], axis=1)

    def corner_other(b):
        for s in range(SUBS):
            for d in range(NX):
                rows = pl.ds(pl.multiple_of(((x + d) % NX) * PART + s * SUB, SUB), SUB)
                await_recv((c10, c01)[b].at[other, rows], cs_s.at[b, s, d], cs_r.at[b, s, d])

    pl.when(apart)(lambda: collect_other(1))
    corner_other(0)

    @pl.when(both(prow > 0, jnp.logical_or(pcol > 1, both(top, pcol == 1))))
    def _():
        right = pivot_rows(1) - product(whole(c10), amid[...])
        tmid[...] = right

        @pl.when(both(below, pcol > 1))
        def _():
            tmid[...] = product(gmid[...], right)


    @pl.when(both(below, pcol > 0))
    def _():
        left_near[...] = px1[:, pl.ds(near, HALF)] - product(bmid[...], c01[h])

        @pl.when(pcol > 1)
        def _():
            f1[...] = f1[...] - product(left_near[...], tmid[pl.ds(near, HALF)])

    corner_other(1)
    def first_block():
        @pl.when(pcol == 0)
        def _():
            out_ref[...] = pivot_rows(0)

        @pl.when(pcol > 0)
        def _():
            out_ref[...] = ur0[...]

    def second_block():
        @pl.when(pcol == 0)
        def _():
            out_ref[...] = product(whole(c10), u0[...])

        @pl.when(pcol > 0)
        def _():
            @pl.when(pcol == 1)
            def _():
                out_ref[...] = tmid[...]

            @pl.when(pcol > 1)
            def _():
                out_ref[...] = product(l1[...], tmid[...])

    def trailing():
        @pl.when(pcol == 0)
        def _():
            out_ref[...] = product(px0[...], u0[...])

        @pl.when(pcol > 0)
        def _():
            left_far = px1[:, pl.ds(far, HALF)] - product(bmid[...], c01[other])

            @pl.when(pcol == 1)
            def _():
                out_ref[...] = product(left_near[...], u1[pl.ds(near, HALF)]) + product(left_far, u1[pl.ds(far, HALF)])

            @pl.when(pcol > 1)
            def _():
                out_ref[...] = f1[...] - product(left_far, tmid[pl.ds(far, HALF)])

    pl.when(prow == 0)(first_block)
    pl.when(prow == 1)(second_block)
    pl.when(below)(trailing)

    pending.extend(late)
    drain()


def on_device(
    matrix, pivots_first, pivots_second, lower_first, upper_first, lower_second, upper_second
):
    vmem = pl.BlockSpec(memory_space=pltpu.VMEM)
    anywhere = pl.BlockSpec(memory_space=pl.ANY)
    block = (NB, NB)
    dma = pltpu.SemaphoreType.DMA
    nu = 2 * WCH + 2 * SUBS
    return pl.pallas_call(
        kernel,
        out_shape=jax.ShapeDtypeStruct(block, F32),
        in_specs=[vmem] * 3 + [anywhere] * 4,
        out_specs=vmem,
        scratch_shapes=[pltpu.VMEM(block, F32)] * 4
        + [
            pltpu.VMEM((2, NB, HALF), F32),
            pltpu.VMEM((2, NB, HALF), F32),
            pltpu.VMEM((2, NB, HALF), F32),
            pltpu.VMEM((2, NB, HALF), F32),
            pltpu.VMEM((2, 2, NB, HALF), F32),
            pltpu.VMEM((2, 2, NB, HALF), F32),
            pltpu.VMEM(block, F32),
            pltpu.VMEM(block, F32),
            pltpu.VMEM(block, F32),
            pltpu.VMEM((2, NB, HALF), F32),
            pltpu.VMEM((2, NB, HALF), F32),
        ]
        + [pltpu.VMEM(block, F32)] * 6
        + [pltpu.VMEM((2, NB, NB), BF16), pltpu.VMEM((2, NB, 1), F32), pltpu.VMEM((NB, 1), F32)]
        + [dma((4,)), dma((2, 2)), dma((2, 2))]
        + [dma((2, RCH))] * 10
        + [
            dma((nu, 2, NX - 1)), dma((nu, 2)),
            dma((nu, 2, 4)), dma((nu, 2)),
            dma((nu, NX - 1)), dma((nu, NX - 1)),
            dma((nu, 4)), dma((nu, 4)),
            dma((2, SUBS, NX)), dma((2, SUBS, NX)),
            dma((2, SUBS, NX)), dma((2, SUBS, NX)),
            pltpu.VMEM(block, F32),
            pltpu.VMEM((NB, HALF), F32),
        ],
        compiler_params=pltpu.CompilerParams(
            collective_id=0, has_side_effects=True, vmem_limit_bytes=56 << 20
        ),
    )(
        matrix, pivots_first.reshape(1, NB), pivots_second.reshape(1, NB),
        lower_first, upper_first, lower_second, upper_second,
    )


def solution(mesh):
    placed = (P("prow", "pcol"), P(), P(), P(), P(), P(), P())
    return jax.shard_map(
        on_device, mesh=mesh, in_specs=placed, out_specs=P("prow", "pcol"), check_vma=False
    )
```

```python
import functools

import jax
import jax.numpy as jnp
from jax import lax
from jax.experimental import pallas as pl
from jax.experimental.pallas import tpu as pltpu
from jax.sharding import PartitionSpec as P

MESH = pl.DeviceIdType.MESH
NB = 512
HALF = NB // 2
NY, NC, NZ, NX = 4, 2, 8, 4
PART = NB // NX
SUBS = 2
SUB = PART // SUBS
WCH = 4
WCOLS = NB // WCH
RCH = 8
RROWS = HALF // 2
LAG = 2
PAIRED = (2, 3, 4, 5, 8, 9, 10, 11)
RETURNED = (0, 1, 2, 3)
F32 = jnp.float32
BF16 = jnp.bfloat16


def dot1(a, b):
    return jnp.dot(a, b, preferred_element_type=F32)


def split2(a):
    high = a.astype(BF16)
    return high, (a - high.astype(F32)).astype(BF16)


def split3(a):
    high = a.astype(BF16)
    rest = a - high.astype(F32)
    mid = rest.astype(BF16)
    return high, mid, (rest - mid.astype(F32)).astype(BF16)


def joined(a, b):
    ah, al = a
    bh, bl = b
    return dot1(ah, bh) + (dot1(ah, bl) + dot1(al, bh))


def product(a, b):
    return joined(split2(a), split2(b))


def keep(ref, value):
    ref[0], ref[1] = split2(value)


def both_parts(ref):
    return ref[0], ref[1]


def pick(onehot, parts):
    high, mid, low = parts
    return dot1(onehot, high) + (dot1(onehot, mid) + dot1(onehot, low))


def onehot_of(source, first):
    lanes = lax.broadcasted_iota(jnp.int32, (NB, NB), 1).astype(F32) + first
    return jnp.where(source == lanes, 1.0, 0.0).astype(BF16)


def kernel(
    w_hbm, pf_ref, ps_ref, l0_hbm, u0_hbm, l1_hbm, u1_hbm, out_ref,
    w_ref, l0, u0, l1, u1, xp, sib, hs, turn, mb, xf, xi, px0, px1, c10, c01, ur0, f1,
    gmid, ulmid, bmid, amid, hot, own, moved, fac_sem, sib_s, sib_r,
    p1_s, p1_r, p2f_s, p2f_r, p2b_s, p2b_r, ms_s, ms_r, xs_s, xs_r,
    a_s, a_r, b_s, b_r, c_s, c_r, r_s, r_r, y_s, y_r, cs_s, cs_r, tmid, left_near,
):
    prow = lax.axis_index("prow")
    pcol = lax.axis_index("pcol")
    y, h = prow // 2, prow % 2
    z, x = pcol // NX, pcol % NX
    other = 1 - h
    top = y == 0
    below = y > 0
    row0 = z == 0
    rooted = pcol < 2
    lead = jnp.where(pcol == 0, 1, 0)

    def at(dy=0, dc=0, dz=0, dx=0):
        return {
            "prow": ((y + dy + NY) % NY) * NC + (h + dc) % NC,
            "pcol": ((z + dz + NZ) % NZ) * NX + (x + dx + NX) % NX,
        }

    sibling = at(dc=1)
    pending = []

    def both(*conds):
        conds = [c for c in conds if c is not None]
        return functools.reduce(jnp.logical_and, conds) if conds else None

    def when(cond, fn):
        if cond is None:
            fn()
        else:
            pl.when(cond)(fn)

    def drain():
        groups = {}
        for cond, copy in pending:
            groups.setdefault(id(cond), (cond, []))[1].append(copy)
        pending.clear()
        for cond, copies in groups.values():

            def run(copies=copies):
                for copy in copies:
                    copy.wait_send()

            when(cond, run)

    known = {}

    def named(name, make):
        if name not in known:
            known[name] = make()
        return known[name]

    def remote(src, dst, ssem, rsem, device):
        return pltpu.make_async_remote_copy(
            src_ref=src, dst_ref=dst, send_sem=ssem, recv_sem=rsem, device_id=device, device_id_type=MESH
        )

    def send(src, dst, ssem, rsem, device, cond=None):
        copy = remote(src, dst, ssem, rsem, device)
        when(cond, copy.start)
        pending.append((cond, copy))

    def await_recv(dst, ssem, rsem, cond=None):
        when(cond, remote(dst, dst, ssem, rsem, sibling).wait_recv)

    load = pltpu.make_async_copy(w_hbm, w_ref, fac_sem.at[4])
    load.start()
    factors = [
        pltpu.make_async_copy(src, dst, fac_sem.at[k])
        for k, (src, dst) in enumerate(((l0_hbm, l0), (u0_hbm, u0), (l1_hbm, l1), (u1_hbm, u1)))
    ]
    for copy in factors:
        copy.start()

    ahead = both(row0, rooted)
    later = jnp.logical_not(ahead)
    column = [at(dc=1), at(dy=1), at(dy=2), at(dy=3)]
    moves = [(0, 1), (0, 2), (0, 3), (1, 0), (2, 0), (-1, 0), (-2, 0)]
    crosswise = []
    for dz, dx in moves:
        theirs = both((z + dz + NZ) % NZ == 0, (x + dx) % NX < 2)
        crosswise.append((at(dz=dz, dx=dx), theirs))
    barrier = pltpu.get_barrier_semaphore()

    def greet(device):
        pl.semaphore_signal(barrier, inc=1, device_id=device, device_id_type=MESH)

    for device in column:
        greet(device)
    for device, theirs in crosswise:
        pl.when(ahead == theirs)(functools.partial(greet, device))

    base = (prow * NB).astype(F32)
    chip = (y * 2 * NB).astype(F32)
    pf_row = pf_ref[...].astype(F32)
    ps_row = ps_ref[...].astype(F32)
    row_id = lax.broadcasted_iota(jnp.int32, (NB, NB), 0).astype(F32)
    col_id = lax.broadcasted_iota(jnp.int32, (NB, NB), 1).astype(F32)
    slot_col = row_id[:, 0:1]
    diagonal = row_id == col_id
    pf_col = jnp.sum(jnp.where(diagonal, pf_row, 0.0), axis=1, keepdims=True)
    ps_col = jnp.sum(jnp.where(diagonal, ps_row, 0.0), axis=1, keepdims=True)
    chained = jnp.sum(jnp.where(ps_col == pf_row, col_id + 1.0, 0.0), axis=1, keepdims=True)
    src1 = jnp.where(chained > 0.0, chained - 1.0, ps_col)
    linked_col = jnp.sum(jnp.where(pf_row == row_id + float(NB), col_id + 1.0, 0.0), axis=1, keepdims=True)
    origin_col = jnp.where(linked_col > 0.0, linked_col - 1.0, slot_col + float(NB))
    linked_row = jnp.sum(jnp.where(pf_col == col_id + float(NB), row_id + 1.0, 0.0), axis=0, keepdims=True)
    origin_row = jnp.where(linked_row > 0.0, linked_row, col_id[0:1] + float(NB + 1))
    again = jnp.sum(jnp.where(pf_col == ps_row, origin_row, 0.0), axis=1, keepdims=True)
    back0 = jnp.where(again > 0.0, again - 1.0, slot_col)
    held = float(2 * NB)
    swap0 = jnp.where(jnp.logical_and(top, pf_col >= held), back0, pf_col)
    swap1 = jnp.where(jnp.logical_and(top, src1 >= held), origin_col, src1)
    far = pl.multiple_of(other * HALF, HALF)
    near = pl.multiple_of(h * HALF, HALF)
    wanted = [onehot_of(jnp.where(lead == stage, swap0, swap1), base) for stage in range(2)]
    load.wait()
    w_far = split3(w_ref[:, pl.ds(far, HALF)])
    for stage in range(2):
        xp[stage] = pick(wanted[stage], w_far)

    @pl.when(ahead)
    def _():
        pl.semaphore_wait(barrier, len(column) + 1)
        for device, theirs in crosswise:
            pl.when(jnp.logical_not(theirs))(functools.partial(greet, device))

    @pl.when(later)
    def _():
        pl.semaphore_wait(barrier, len(column) + len(crosswise))
        for device, theirs in crosswise:
            pl.when(theirs)(functools.partial(greet, device))


    for c in range(2):
        cols = pl.ds(c * WCOLS, WCOLS)
        for stage in range(2):
            sems = (sib_s.at[c, stage], sib_r.at[c, stage])
            send(xp.at[stage, :, cols], sib.at[stage, :, cols], *sems, sibling)
    w_near = split3(w_ref[:, pl.ds(near, HALF)])
    for stage in range(2):
        hs[stage] = pick(wanted[stage], w_near)

    for stage in range(2):
        source = jnp.where(lead == stage, pf_col, src1)
        inside = jnp.logical_and(source >= chip, source < chip + held)
        own[stage] = jnp.where(inside, 1.0, 0.0)

    def add_other(c):
        cols = pl.ds(c * WCOLS, WCOLS)
        for stage in range(2):
            await_recv(sib.at[stage, :, cols], sib_s.at[c, stage], sib_r.at[c, stage])
            hs[stage, :, cols] = hs[stage, :, cols] + sib[stage, :, cols]

    def piece(way, j):
        s, sub = (j // 2) % 2, j % 2
        rows = pl.ds(way * HALF + sub * RROWS, RROWS)
        cols = pl.ds((j // 4) * WCOLS, WCOLS)
        return s, rows, cols

    ring = {}
    for way in range(2):
        dy = 1 - 2 * way
        first = y == 0
        last = y == (3 if way == 0 else 1)
        between = both(below, jnp.logical_not(last))
        whole_ring = jnp.logical_not(rooted)
        forth_cond = jnp.logical_or(last, both(first, whole_ring))
        back_cond = both(last, whole_ring)
        final_cond = jnp.logical_or(top, whole_ring)
        for j in range(RCH):
            where = piece(way, j)
            into = mb.at[(h,) + where]
            done = xf.at[(h,) + where]
            p1 = (p1_s.at[way, j], p1_r.at[way, j])
            copies = dict(
                begin=remote(hs.at[where], into, *p1, at(dy=dy)),
                onward=remote(turn.at[where], into, *p1, at(dy=dy)),
                forth=remote(done, done, p2f_s.at[way, j], p2f_r.at[way, j], at(dy=dy)),
                back=remote(done, done, p2b_s.at[way, j], p2b_r.at[way, j], at(dy=-dy)),
                raw=remote(into, into, ms_s.at[way, j], ms_r.at[way, j], sibling),
                final=remote(done, done, xs_s.at[way, j], xs_r.at[way, j], sibling),
            )
            ring[way, j] = copies
            pending.append((first, copies["begin"]))
            pending.append((between, copies["onward"]))
            pending.append((forth_cond, copies["forth"]))
            pending.append((back_cond, copies["back"]))
            pending.append((below, copies["raw"]))
            pending.append((final_cond, copies["final"]))

    def first_pass(way, j, hop):
        copies = ring[way, j]
        where = piece(way, j)
        s, rows, cols = where
        copies["onward"].wait_recv()
        copies["raw"].start()
        merged = jnp.where(own[s, rows] > 0.0, hs[where], mb[(h,) + where])
        if hop < NY - 1:
            turn[where] = merged
            copies["onward"].start()
        else:
            xf[(h,) + where] = merged
            copies["forth"].start()

            def others():
                copies["back"].start()
                copies["final"].start()

            pl.when(jnp.logical_not(rooted))(others)

    def second_pass(way, j, hop):
        copies = ring[way, j]
        spread_on = jnp.logical_not(rooted)
        if hop == 0:
            copies["forth"].wait_recv()
            when(spread_on, copies["forth"].start)
            copies["final"].start()
        else:

            def arrive():
                copies["back" if hop == 2 else "forth"].wait_recv()
                copies["final"].start()

            when(spread_on, arrive)

    events = {}
    for v in range(NY):
        for way in range(2):
            hop = v if way == 0 else (NY - v) % NY
            for j in range(RCH):
                if hop > 0:
                    events.setdefault((LAG * hop + j, v), []).append((first_pass, way, j, hop))
                if hop < 3:
                    lag = {0: 4, 1: 5, 2: 4}[hop]
                    events.setdefault((LAG * lag + j, v), []).append((second_pass, way, j, hop))

    def slots(begin, end):
        for v in range(NY):
            todo = [e for key in range(begin, end) for e in events.get((key, v), ())]

            def run(todo=todo):
                for fn, way, j, hop in todo:
                    fn(way, j, hop)

            if todo:
                pl.when(y == v)(run)

    def begin_ring(c):
        for j in range(4 * c, 4 * c + 4):
            for way in range(2):
                ring[way, j]["begin"].start()

    def find_rows():
        src1_row = jnp.sum(jnp.where(pf_col == ps_row, row_id + 1.0, 0.0), axis=0, keepdims=True)
        src1_row = jnp.where(src1_row > 0.0, src1_row - 1.0, ps_row)
        count = jnp.zeros((NB, 1), F32)
        for stage in range(2):
            source = jnp.where(lead == stage, pf_row, src1_row)
            mark = jnp.where(source == base + row_id, 1.0, 0.0)
            hot[stage] = mark.astype(BF16)
            count += jnp.sum(mark, axis=1, keepdims=True)
        moved[...] = count

    def place(c):
        for way in range(2):
            for j in range(4 * c, 4 * c + 4):
                ref = mb.at[(other,) + piece(way, j)]
                await_recv(ref, ms_s.at[way, j], ms_r.at[way, j])
        cols = pl.ds(c * WCOLS, WCOLS)
        incoming = jnp.zeros((NB, 2 * WCOLS), F32)
        for stage in range(2):
            rows = jnp.concatenate([mb[0, stage, :, cols], mb[1, stage, :, cols]], axis=1)
            incoming += pick(hot[stage], split3(rows))
        for side in range(2):
            there = pl.ds(side * HALF + c * WCOLS, WCOLS)
            placed = jnp.where(moved[...] > 0.0, incoming[:, side * WCOLS:(side + 1) * WCOLS], w_ref[:, there])
            xi[:, there] = placed

    def place_panel(c):
        @pl.when(both(below, rooted))
        def _():
            place(c)
            for side in range(2):
                there = pl.ds(side * HALF + c * WCOLS, WCOLS)

                @pl.when(pcol == 0)
                def _():
                    px0[:, there] = xi[:, there]

                @pl.when(pcol == 1)
                def _():
                    px1[:, there] = xi[:, there]

    def place_rest(c):
        pl.when(both(below, jnp.logical_not(rooted)))(lambda: place(c))

    def collect_other(stage):
        for way in range(2):
            for j in range(RCH):
                if piece(way, j)[0] == stage:
                    ref = xf.at[(other,) + piece(way, j)]
                    await_recv(ref, xs_s.at[way, j], xs_r.at[way, j])

    units = [(b, s) for s in (0, 2, 1, 3) for b in range(2)] + [(b, s) for b in (2, 3) for s in range(SUBS)]

    corner10 = tuple(range(2 * WCH, 2 * WCH + SUBS))
    corner01 = tuple(range(2 * WCH + SUBS, 2 * WCH + 2 * SUBS))
    corners = corner10 + corner01

    def rows_of(unit, part, half=None):
        b, sub = unit
        count = PART if b < 2 else SUB
        first = part * PART + (0 if b < 2 else sub * SUB)
        if half is not None:
            count = count // 2
            first = first + half * count
        rows = pl.ds(pl.multiple_of(first, count), count)
        if b < 2:
            return (px0, px1)[b].at[rows, pl.ds(sub * WCOLS, WCOLS)]
        return (c10, c01)[b - 2].at[h, rows]

    def parts_of(u, column):
        return (column % NX, (column + 2) % NX) if u in PAIRED else (column % NX,)

    tests = {
        None: None, "row0": row0, "far": z != 0, "forks": jnp.logical_or(z == 2, z == 6),
        "rise": jnp.logical_or(jnp.logical_or(z == 2, z == 6), z == 3),
    }
    for root in range(2):
        tests["root", root] = pcol == root
        tests["apart", root] = pcol != root
        tests["enter", root] = both(row0, x != root)
        for level in (1, 7):
            tests["edge", root, level] = both(z == level, x != root)
        for d in range(1, NX):
            tests["away", root, d] = jnp.logical_not(both(row0, (x + d) % NX == root))

    def unit_steps(u):
        unit = units[u]
        root = unit[0] % 2
        shared = unit[0] >= 2
        first, later, last = [], [], []

        def put(steps, src, ssem, rsem, device, cond):
            copy = remote(src, src, ssem, rsem, device)
            steps.append((cond, copy.start))
            whole = named((shared, cond), lambda: both(top if shared else below, tests[cond]))
            pending.append((whole, copy))

        def take(steps, ref, ssem, rsem, cond):
            steps.append((cond, remote(ref, ref, ssem, rsem, sibling).wait_recv))

        def across(steps, part, slot):
            ref = rows_of(unit, part)
            sems = (unit[0] - 2, unit[1], slot)
            put(steps, ref, cs_s.at[sems], cs_r.at[sems], sibling, None)
            put(steps, ref, y_s.at[sems], y_r.at[sems], at(dy=1 if slot < 2 else -1), None)

        for d in (1, 3, 2):
            for slot, part in enumerate(parts_of(u, root + d)):
                put(first, rows_of(unit, part), a_s.at[u, slot, d - 1], a_r.at[u, slot], at(dx=d), ("root", root))

        for slot, part in enumerate(parts_of(u, x)):
            ref = rows_of(unit, part)
            take(later, ref, a_s.at[u, slot, 0], a_r.at[u, slot], ("enter", root))
            take(later, ref, b_s.at[u, slot, 0], b_r.at[u, slot], "far")
            for k, (dz, cond) in enumerate((
                (2, "row0"), (-2, "row0"), (1, "rise"), (-1, "forks"),
            )):
                put(later, ref, b_s.at[u, slot, k], b_r.at[u, slot], at(dz=dz), cond)
        ref = rows_of(unit, x)
        for d in (1, 3) if u in PAIRED else (1, 3, 2):
            away = "far" if u in RETURNED else ("away", root, d)
            put(later, ref, c_s.at[u, d - 1], c_r.at[u, d - 1], at(dx=d), away)
        if shared:
            for slot, part in enumerate(parts_of(u, x)):
                across(later, part, 2 * slot)

        for d in (1, 3) if u in PAIRED else (1, 3, 2):
            part = (x + d) % NX
            take(last, rows_of(unit, part), c_s.at[u, 3 - d], c_r.at[u, 3 - d], "far" if u in RETURNED else ("apart", root))
            pieces = {1: ((None, 1, 0),), 3: ((None, 7, 1),), 2: ((0, 1, 2), (1, 7, 3))}[d]
            for half, level, slot in pieces if u in RETURNED else ():
                ref = rows_of(unit, part, half)
                dz = 1 if level == 7 else -1
                put(last, ref, r_s.at[u, slot], r_r.at[u, slot], at(dz=dz), ("edge", root, level))
                take(last, ref, r_s.at[u, slot], r_r.at[u, slot], ("enter", root))
            if shared:
                across(last, part, d)
        return first, later, last

    steps_of = [unit_steps(u) for u in range(2 * WCH + 2 * SUBS)]

    def carry(phase, chosen, role=None):
        for wanted, plane in ((lambda u: units[u][0] < 2, below), (lambda u: units[u][0] >= 2, top)):
            group = [u for u in chosen if wanted(u)]

            def run(group=group):
                merged = []
                for u in group:
                    for cond, act in steps_of[u][phase]:
                        if merged and merged[-1][0] == cond:
                            merged[-1][1].append(act)
                        else:
                            merged.append((cond, [act]))
                for cond, acts in merged:
                    when(tests[cond], lambda acts=acts: [act() for act in acts] and None)

            if group:
                when(both(plane, role), run)

    scatter = functools.partial(carry, 0)
    spread = functools.partial(carry, 1)
    gather = functools.partial(carry, 2)
    is_root = both(row0, rooted)
    is_entry = both(row0, jnp.logical_not(rooted))
    is_fork = jnp.logical_or(z == 2, z == 6)
    is_edge = jnp.logical_or(z == 1, z == 7)
    is_inner = jnp.logical_not(is_edge)
    is_leaf = both(z != 0, jnp.logical_not(is_fork))
    is_far = z != 0

    handed = {}
    late = []
    for u in corners:
        b, s = units[u][0] - 2, units[u][1]
        for slot in range(NX):
            ref = rows_of(units[u], (x + slot) % NX)
            sems = (b, s, slot)
            onward = remote(ref, ref, y_s.at[sems], y_r.at[sems], at(dy=1 if slot < 2 else -1))
            across = remote(ref, ref, cs_s.at[sems], cs_r.at[sems], sibling)
            handed[u, slot] = onward, across
            middle = named(("middle", slot < 2), lambda: jnp.logical_or(y == 2, y == (1 if slot < 2 else 3)))
            late.append((middle, onward))
            late.append((below, across))

    def hand_down(stage):
        for v in range(1, NY):
            near, away = ((2, 3), (0, 1)) if v == 3 else ((0, 1), (2, 3))
            if v == 2:
                todo = (
                    [(u, slot) for u in corners for slot in (0, 2)],
                    [(u, slot) for u in corners for slot in (1, 3)],
                    [],
                )[stage]
            else:
                todo = (
                    [(u, near[0]) for u in corners],
                    [(u, near[1]) for u in corners],
                    [(u, slot) for b in (corner10, corner01) for slot in away for u in b],
                )[stage]

            def run(todo=todo, v=v):
                for u, slot in todo:
                    onward, across = handed[u, slot]
                    onward.wait_recv()
                    if v == 2 or v == (1 if slot < 2 else 3):
                        onward.start()
                    across.start()

            if todo:
                pl.when(y == v)(run)

    def spread_own(chosen, mine):
        for column in range(2):
            spread([u for u in chosen if (units[u][0] % 2 == column) == mine], both(row0, pcol == column))

    panel = (tuple(range(0, 4)), tuple(range(4, 8)))

    def keep_corner(corner):
        corner[h] = xf[h, 0]

    def pivot_rows(q):
        stage = jnp.where(lead == 1, 1 - q, q)
        return jnp.concatenate([xf[0, stage], xf[1, stage]], axis=1)

    for c in range(2):
        add_other(c)
        pl.when(top)(functools.partial(begin_ring, c))
    slots(0, 4)
    pl.when(below)(find_rows)
    slots(4, 6)
    for copy in factors:
        copy.wait()

    @pl.when(both(below, jnp.logical_not(rooted)))
    def _():
        keep(gmid, product(u1[...], l1[...]))
        keep(ulmid, product(u0[...], l0[...]))

    slots(6, 10)
    place_panel(0)
    pl.when(ahead)(lambda: pl.semaphore_wait(barrier, len(crosswise) - 1))
    scatter(panel[0], is_root)
    spread_own(panel[0], True)
    spread(panel[0], is_entry)
    slots(10, 14)
    spread_own(panel[0], False)
    place_panel(1)
    scatter(panel[1], is_root)
    spread_own(panel[1], True)
    spread(panel[0], is_fork)
    slots(14, 16)
    pl.when(both(top, pcol == 0))(lambda: keep_corner(c10))
    pl.when(both(top, pcol == 1))(lambda: keep_corner(c01))
    scatter(corners, is_root)
    spread_own(corners, True)
    spread_own(panel[1], False)
    spread(panel[1], is_entry)
    spread(panel[0], is_leaf)
    spread_own(corners, False)
    spread(corners, is_entry)
    spread(panel[1], is_fork)
    slots(16, 18)
    place_rest(0)
    spread(panel[1], is_leaf)
    spread(corner10, is_far)
    spread(corner01, is_far)
    gather(corner10)
    gather(corner01)
    gather(panel[0], is_edge)
    hand_down(0)
    place_rest(1)
    hand_down(1)
    apart = jnp.logical_or(top, jnp.logical_not(rooted))
    pl.when(apart)(lambda: collect_other(0))

    @pl.when(both(pcol > 0, apart))
    def _():
        ur0[...] = product(l0[...], pivot_rows(0))
        keep(amid, product(u0[...], ur0[...]))

    gather(panel[0], is_inner)
    gather(panel[1])
    def early():
        @pl.when(pcol > 0)
        def _():
            @pl.when(pcol == 1)
            def _():
                keep(ulmid, product(u0[...], l0[...]))

            panel_parts = split2(px0[...])
            keep(bmid, joined(panel_parts, both_parts(ulmid)))

            @pl.when(pcol > 1)
            def _():
                f1[...] = xi[...] - joined(panel_parts, both_parts(amid))

    pl.when(below)(early)
    drain()
    hand_down(2)

    def whole(ref):
        return jnp.concatenate([ref[0], ref[1]], axis=1)

    def corner_other(b):
        for s in range(SUBS):
            for d in range(NX):
                rows = pl.ds(pl.multiple_of(((x + d) % NX) * PART + s * SUB, SUB), SUB)
                await_recv((c10, c01)[b].at[other, rows], cs_s.at[b, s, d], cs_r.at[b, s, d])

    pl.when(apart)(lambda: collect_other(1))
    corner_other(0)

    @pl.when(both(prow > 0, jnp.logical_or(pcol > 1, both(top, pcol == 1))))
    def _():
        right = pivot_rows(1) - joined(split2(whole(c10)), both_parts(amid))
        tmid[...] = right

        @pl.when(both(below, pcol > 1))
        def _():
            tmid[...] = joined(both_parts(gmid), split2(right))


    @pl.when(both(below, pcol > 0))
    def _():
        left_near[...] = px1[:, pl.ds(near, HALF)] - joined(both_parts(bmid), split2(c01[h]))

        @pl.when(pcol > 1)
        def _():
            f1[...] = f1[...] - product(left_near[...], tmid[pl.ds(near, HALF)])

    corner_other(1)
    def first_block():
        @pl.when(pcol == 0)
        def _():
            out_ref[...] = pivot_rows(0)

        @pl.when(pcol > 0)
        def _():
            out_ref[...] = ur0[...]

    def second_block():
        @pl.when(pcol == 0)
        def _():
            out_ref[...] = product(whole(c10), u0[...])

        @pl.when(pcol > 0)
        def _():
            @pl.when(pcol == 1)
            def _():
                out_ref[...] = tmid[...]

            @pl.when(pcol > 1)
            def _():
                out_ref[...] = product(l1[...], tmid[...])

    def trailing():
        @pl.when(pcol == 0)
        def _():
            out_ref[...] = product(px0[...], u0[...])

        @pl.when(pcol > 0)
        def _():
            left_far = px1[:, pl.ds(far, HALF)] - joined(both_parts(bmid), split2(c01[other]))

            @pl.when(pcol == 1)
            def _():
                out_ref[...] = product(left_near[...], u1[pl.ds(near, HALF)]) + product(left_far, u1[pl.ds(far, HALF)])

            @pl.when(pcol > 1)
            def _():
                out_ref[...] = f1[...] - product(left_far, tmid[pl.ds(far, HALF)])

    pl.when(prow == 0)(first_block)
    pl.when(prow == 1)(second_block)
    pl.when(below)(trailing)

    pending.extend(late)
    drain()


def on_device(
    matrix, pivots_first, pivots_second, lower_first, upper_first, lower_second, upper_second
):
    vmem = pl.BlockSpec(memory_space=pltpu.VMEM)
    anywhere = pl.BlockSpec(memory_space=pl.ANY)
    block = (NB, NB)
    dma = pltpu.SemaphoreType.DMA
    nu = 2 * WCH + 2 * SUBS
    return pl.pallas_call(
        kernel,
        out_shape=jax.ShapeDtypeStruct(block, F32),
        in_specs=[anywhere] + [vmem] * 2 + [anywhere] * 4,
        out_specs=vmem,
        scratch_shapes=[pltpu.VMEM(block, F32)] * 5
        + [
            pltpu.VMEM((2, NB, HALF), F32),
            pltpu.VMEM((2, NB, HALF), F32),
            pltpu.VMEM((2, NB, HALF), F32),
            pltpu.VMEM((2, NB, HALF), F32),
            pltpu.VMEM((2, 2, NB, HALF), F32),
            pltpu.VMEM((2, 2, NB, HALF), F32),
            pltpu.VMEM(block, F32),
            pltpu.VMEM(block, F32),
            pltpu.VMEM(block, F32),
            pltpu.VMEM((2, NB, HALF), F32),
            pltpu.VMEM((2, NB, HALF), F32),
        ]
        + [pltpu.VMEM(block, F32)] * 2
        + [pltpu.VMEM((2, NB, NB), BF16)] * 5
        + [pltpu.VMEM((2, NB, 1), F32), pltpu.VMEM((NB, 1), F32)]
        + [dma((5,)), dma((2, 2)), dma((2, 2))]
        + [dma((2, RCH))] * 10
        + [
            dma((nu, 2, NX - 1)), dma((nu, 2)),
            dma((nu, 2, 4)), dma((nu, 2)),
            dma((nu, NX - 1)), dma((nu, NX - 1)),
            dma((nu, 4)), dma((nu, 4)),
            dma((2, SUBS, NX)), dma((2, SUBS, NX)),
            dma((2, SUBS, NX)), dma((2, SUBS, NX)),
            pltpu.VMEM(block, F32),
            pltpu.VMEM((NB, HALF), F32),
        ],
        compiler_params=pltpu.CompilerParams(
            collective_id=0, has_side_effects=True, vmem_limit_bytes=56 << 20
        ),
    )(
        matrix, pivots_first.reshape(1, NB), pivots_second.reshape(1, NB),
        lower_first, upper_first, lower_second, upper_second,
    )


def solution(mesh):
    placed = (P("prow", "pcol"), P(), P(), P(), P(), P(), P())
    return jax.shard_map(
        on_device, mesh=mesh, in_specs=placed, out_specs=P("prow", "pcol"), check_vma=False
    )
```
